256 devices in a mesh: wide: 32 (over x_lo, z, core), narrow: 8 (over y, x_hi).
Axes of the slice: x: 4 (x_hi: 2, x_lo: 2; x = x_hi * 2 + x_lo), y: 4, z: 8, core: 2. Of those that a mesh axis runs over, the one named last changes fastest.
Arguments:
- activations: bfloat16 [256, 256, 32, 256], P('wide', 'narrow'), may hold values from -6 to 6
- cotangent: bfloat16 [256, 256, 32, 256], P('wide', 'narrow'), may hold values from -6 to 6
- point_weight: bfloat16 [32, 32], replicated, may hold values from -1 to 1
- bias: float32 [32], replicated, may hold values from -3 to 3
- spectral_weight: bfloat16 [2, 32, 32, 16, 32, 32], P(None, 'wide', 'narrow'), may hold values from -6 to 6
Outputs:
- input_grad: bfloat16 [256, 256, 32, 256], P('wide', 'narrow')
- point_grad: float32 [32, 32], replicated
- bias_grad: float32 [32], replicated
- spectral_grad: float32 [2, 32, 32, 16, 32, 32], P(None, 'wide', 'narrow')
The draws below stay inside these ranges and needn't reach their ends.
All inputs are finite; a program needn't handle non-finite values.
Results may differ from the reference program's by a relative error of at most 0.0065.
Values sent between devices are 32-bit elements; how exact they have to be, the bound alone decides.
A program may use at most 128 MiB of HBM per device.

```python
import math
import jax
import jax.numpy as jnp
from jax import lax

C = 32
M = 16
NZ = 256
NX = 256
NY = 256


def level_of(key, shape, cuts, low, high):
    def one(axis_at, shards_of):
        steps = jax.random.uniform(jax.random.fold_in(jax.random.fold_in(key, 6), axis_at), (shards_of,), jnp.float32, low / len(cuts), high / len(cuts))
        return jnp.repeat(jnp.exp(steps), shape[axis_at] // shards_of).reshape((-1,) + (1,) * (len(shape) - axis_at - 1))

    gain = one(*cuts[0])
    for cut in cuts[1:]:
        gain = gain * one(*cut)
    return gain


def bell_draw(own_key, shape, width, limit, pieces=(), held_as=jnp.bfloat16):
    entries = jax.random.normal(own_key, shape, jnp.float32) * width
    if len(pieces) > 0:
        entries = level_of(own_key, shape, pieces, -0.22, 0.18) * entries
    return jnp.clip(entries, min=-limit, max=limit).astype(held_as)


def setup_inputs(seed: int = 0) -> dict:
    splits = jax.random.split(jax.random.key(seed), 6)
    activations = bell_draw(splits[0], (NX, NY, C, NZ), 1.0, 6.0, ((0, 32), (1, 8)))
    cotangent = bell_draw(splits[1], (NX, NY, C, NZ), 1.0, 6.0, ((0, 32), (1, 8)))
    point_weight = bell_draw(splits[2], (C, C), C ** -0.5, 1.0)
    bias = bell_draw(splits[3], (C,), 0.5, 3.0, (), jnp.float32)
    spectral_weight = bell_draw(splits[4], (2, 2 * M, 2 * M, M, C, C), 1.0, 6.0, ((1, 32), (2, 8)))
    return dict(activations=activations, cotangent=cotangent, point_weight=point_weight, bias=bias, spectral_weight=spectral_weight)


precise = lax.Precision.HIGHEST

def contract(form, left, right):
    return jnp.einsum(form, left, right, precision=precise, preferred_element_type=jnp.float32)

def kept_freq(index, length, half):
    return jnp.where(index < half, index, length - 2 * half + index)

def phase_tables(freqs, cells, length):
    product = freqs[:, None] * cells[None, :] % length
    angle = product.astype(jnp.float32) * (2.0 * math.pi / length)
    return (jnp.cos(angle), jnp.sin(angle))

def rotate(real_part, imag_part, cosine, sine, sign_value, form):
    first = contract(form, real_part, cosine) - sign_value * contract(form, imag_part, sine)
    second = contract(form, imag_part, cosine) + sign_value * contract(form, real_part, sine)
    return (first, second)

def depth_forward(field, modes):
    length = field.shape[3]
    cosine, sine = phase_tables(jnp.arange(modes, dtype=jnp.int32), jnp.arange(length, dtype=jnp.int32), length)
    values = field.astype(jnp.float32)
    real_part = contract('abcz,kz->abck', values, cosine)
    imag_part = -contract('abcz,kz->abck', values, sine)
    shape = (field.shape[0], field.shape[1], -1)
    return (real_part.reshape(shape), imag_part.reshape(shape))

def depth_inverse(real_part, imag_part, depth_weights, length):
    modes = depth_weights.shape[0]
    shape = (real_part.shape[0], real_part.shape[1], real_part.shape[2] // modes, modes)
    cosine, sine = phase_tables(jnp.arange(modes, dtype=jnp.int32), jnp.arange(length, dtype=jnp.int32), length)
    return contract('abck,kz->abcz', real_part.reshape(shape), cosine * depth_weights[:, None]) - contract('abck,kz->abcz', imag_part.reshape(shape), sine * depth_weights[:, None])

def mix_modes(coeffs, weight):
    lead_x, lead_y = (coeffs.shape[0], coeffs.shape[1])
    modes = weight.shape[3]
    split = coeffs.reshape(lead_x, lead_y, 2, -1, modes)
    factor = weight.astype(jnp.float32)
    real_part = contract('pqck,pqkco->pqok', split[:, :, 0], factor[0]) - contract('pqck,pqkco->pqok', split[:, :, 1], factor[1])
    imag_part = contract('pqck,pqkco->pqok', split[:, :, 0], factor[1]) + contract('pqck,pqkco->pqok', split[:, :, 1], factor[0])
    return jnp.stack((real_part, imag_part), axis=2).reshape(lead_x, lead_y, 2, -1)

def weight_terms(coeffs, grads, weight):
    lead_x, lead_y = (coeffs.shape[0], coeffs.shape[1])
    modes = weight.shape[3]
    split_c = coeffs.reshape(lead_x, lead_y, 2, -1, modes)
    split_g = grads.reshape(lead_x, lead_y, 2, -1, modes)
    form = 'pqck,pqok->pqkco'
    grad_real = contract(form, split_c[:, :, 0], split_g[:, :, 0]) + contract(form, split_c[:, :, 1], split_g[:, :, 1])
    grad_imag = contract(form, split_c[:, :, 0], split_g[:, :, 1]) - contract(form, split_c[:, :, 1], split_g[:, :, 0])
    factor = weight.astype(jnp.float32)
    back = 'pqok,pqkco->pqck'
    back_real = contract(back, split_g[:, :, 0], factor[0]) + contract(back, split_g[:, :, 1], factor[1])
    back_imag = contract(back, split_g[:, :, 1], factor[0]) - contract(back, split_g[:, :, 0], factor[1])
    coeff_grad = jnp.stack((back_real, back_imag), axis=2).reshape(lead_x, lead_y, 2, -1)
    return (jnp.stack((grad_real, grad_imag), axis=0), coeff_grad)

def reference(activations, cotangent, point_weight, bias, spectral_weight):
    scale = 1.0 / math.sqrt(NX * NY * NZ)
    block = 8
    number = NX // block
    slabs = activations.reshape(number, block, NY, C, NZ)
    grads_in = cotangent.reshape(number, block, NY, C, NZ)
    starts = jnp.arange(number, dtype=jnp.int32) * block
    all_modes = jnp.arange(2 * M, dtype=jnp.int32)
    cos_y, sin_y = phase_tables(kept_freq(all_modes, NY, M), jnp.arange(NY, dtype=jnp.int32), NY)
    freq_x = kept_freq(all_modes, NX, M)
    depth_weights = jnp.where(jnp.arange(M, dtype=jnp.int32) == 0, 1.0, 2.0).astype(jnp.float32)
    unit_weights = jnp.ones((M,), jnp.float32)
    point_full = point_weight.astype(jnp.float32)

    def plane_forward(real_part, imag_part, start):
        cells = start + jnp.arange(block, dtype=jnp.int32)
        cos_x, sin_x = phase_tables(freq_x, cells, NX)
        re_y, im_y = rotate(real_part, imag_part, cos_y, sin_y, -1.0, 'ayf,ky->kaf')
        re_x, im_x = rotate(re_y, im_y, cos_x, sin_x, -1.0, 'qaf,ka->kqf')
        return jnp.stack((re_x, im_x), axis=2)

    def plane_inverse(modes, start):
        cells = start + jnp.arange(block, dtype=jnp.int32)
        cos_x, sin_x = phase_tables(freq_x, cells, NX)
        re_x, im_x = rotate(modes[:, :, 0], modes[:, :, 1], cos_x, sin_x, 1.0, 'kqf,ka->aqf')
        return rotate(re_x, im_x, cos_y, sin_y, 1.0, 'akf,ky->ayf')

    def first_pass(carry, item):
        slab, start = item
        real_part, imag_part = depth_forward(slab, M)
        return (carry + plane_forward(real_part, imag_part, start), None)
    initial = jnp.zeros((2 * M, 2 * M, 2, C * M), jnp.float32)
    total, _ = lax.scan(first_pass, initial, (slabs, starts))
    coeffs = total * scale
    mixed = mix_modes(coeffs, spectral_weight)

    def pre_gradient(slab, gradient, start):
        real_part, imag_part = plane_inverse(mixed, start)
        spectral = depth_inverse(real_part, imag_part, depth_weights, NZ) * scale
        point = contract('abcz,co->aboz', slab.astype(jnp.float32), point_full)
        preact = spectral + point + bias[None, None, :, None]
        _, pullback = jax.vjp(jax.nn.gelu, preact)
        return pullback(gradient.astype(jnp.float32))[0].astype(jnp.bfloat16)

    def second_pass(carry, item):
        slab, gradient, start = item
        pre_grad = pre_gradient(slab, gradient, start)
        real_part, imag_part = depth_forward(pre_grad, M)
        modes_sum, weight_sum, bias_sum = carry
        modes_sum = modes_sum + plane_forward(real_part, imag_part, start)
        weight_sum = weight_sum + contract('abcz,aboz->co', slab.astype(jnp.float32), pre_grad.astype(jnp.float32))
        bias_sum = bias_sum + lax.optimization_barrier(jnp.sum(pre_grad.astype(jnp.float32), axis=(0, 1, 3)))
        return ((modes_sum, weight_sum, bias_sum), None)
    carry = (initial, jnp.zeros((C, C), jnp.float32), jnp.zeros((C,), jnp.float32))
    (modes_sum, weight_sum, bias_sum), _ = lax.scan(second_pass, carry, (slabs, grads_in, starts))
    grads = ((modes_sum * scale).reshape(2 * M, 2 * M, 2, C, M) * depth_weights).reshape(2 * M, 2 * M, 2, C * M)
    spectral_grad, coeff_grad = weight_terms(coeffs, grads, spectral_weight)

    def third_pass(item):
        slab, gradient, start = item
        pre_grad = pre_gradient(slab, gradient, start)
        real_part, imag_part = plane_inverse(coeff_grad, start)
        back = depth_inverse(real_part, imag_part, unit_weights, NZ) * scale
        point = contract('aboz,co->abcz', pre_grad.astype(jnp.float32), point_full)
        return (point + back).astype(jnp.bfloat16)
    input_grad = lax.map(third_pass, (slabs, grads_in, starts)).reshape(NX, NY, C, NZ)
    return (input_grad, weight_sum * scale, bias_sum * scale, spectral_grad)
```

```python
import functools
import math

import jax
import jax.numpy as jnp
import ml_dtypes
import numpy as np
from jax import lax
from jax.experimental import pallas as pl
from jax.experimental.pallas import tpu as pltpu
from jax.sharding import PartitionSpec as P

WIDE = 32
NARROW = 8
M = 16
C = 32
NZ = 256
XL = 8
YL = 32
KY = 4
SCALE = 1.0 / 4096.0

F32 = jnp.float32
BF16 = jnp.bfloat16


def kept(j):
    return np.where(j < 16, j, 224 + j)


def trig(freqs, cells):
    angle = (np.outer(freqs, cells) % 256) * (2.0 * math.pi / 256.0)
    return np.cos(angle), np.sin(angle)


def split_np(table):
    hi = table.astype(np.float32).astype(ml_dtypes.bfloat16)
    lo = (table - hi.astype(np.float64)).astype(np.float32).astype(ml_dtypes.bfloat16)
    return hi, lo


@functools.lru_cache(maxsize=None)
def tables():
    freqs = kept(np.arange(32))
    cos_a, sin_a = trig(freqs, np.arange(256))
    cos_z, sin_z = trig(np.arange(M), np.arange(NZ))
    eye_x = np.eye(XL)
    cy = cos_a.reshape(NARROW, KY, NARROW, YL)
    sy = sin_a.reshape(NARROW, KY, NARROW, YL)
    both = np.stack((cy, sy))
    yf = np.einsum("dtkny,xu->ntkxudy", both, eye_x).reshape(NARROW, 256, 512)
    both = np.stack((cy, -sy))
    yi = np.einsum("dtkny,xu->nxydktu", both, eye_x).reshape(NARROW, 256, 512)
    xf = np.concatenate((cos_a, sin_a), axis=1) * SCALE
    xi = np.concatenate((cos_a.T, -sin_a.T), axis=1)
    zf = np.tile(np.concatenate((cos_z, -sin_z), axis=0).T, (1, 4))
    depth = np.where(np.arange(M) == 0, 1.0, 2.0)[:, None]

    def inverse_z(weights):
        one = np.concatenate((cos_z * weights, -sin_z * weights), axis=0) * SCALE
        full = np.zeros((4, 128, NZ))
        for g in range(4):
            full[g, g * 32 : (g + 1) * 32] = one
        hi, lo = split_np(full)
        return np.concatenate((hi, hi, lo), axis=1)

    return dict(
        yf=np.stack(split_np(yf), axis=1),
        yi=np.stack(split_np(yi), axis=1),
        xf=np.stack(split_np(xf)),
        xi=np.stack(split_np(xi)),
        zf=np.concatenate(split_np(zf), axis=1),
        ziw=inverse_z(depth),
        zi1=inverse_z(np.ones((M, 1))),
    )


def dot(a, b):
    return jnp.dot(a, b, preferred_element_type=F32)


def halves(x):
    hi = x.astype(BF16)
    return hi, (x - hi.astype(F32)).astype(BF16)


def dot3(table, index, hi, lo):
    t_hi = table[index, 0] if index is not None else table[0]
    t_lo = table[index, 1] if index is not None else table[1]
    return dot(t_hi, hi) + (dot(t_hi, lo) + dot(t_lo, hi))


def turn(x):
    lane = lax.broadcasted_iota(jnp.int32, x.shape, x.ndim - 1)
    real = lax.rem(lane, 32) < 16
    return jnp.where(real, pltpu.roll(x, 112, x.ndim - 1), -pltpu.roll(x, 16, x.ndim - 1))


def remote(src, dst, send, recv, device):
    return pltpu.make_async_remote_copy(
        src_ref=src,
        dst_ref=dst,
        send_sem=send,
        recv_sem=recv,
        device_id=device,
        device_id_type=pl.DeviceIdType.MESH,
    )


def greet(n, w):
    barrier = pltpu.get_barrier_semaphore()

    def one(axis, me, size):
        def body(k, carry):
            pl.semaphore_signal(
                barrier,
                inc=1,
                device_id={axis: lax.rem(me + k, size)},
                device_id_type=pl.DeviceIdType.MESH,
            )
            return carry

        lax.fori_loop(1, size, body, 0)

    one("narrow", n, NARROW)
    one("wide", w, WIDE)
    return barrier


def greeted(barrier):
    pl.semaphore_wait(barrier, NARROW + WIDE - 2)


def others(me, size, fn):
    def body(k, carry):
        fn(lax.rem(me + k, size))
        return carry

    lax.fori_loop(1, size, body, 0)


def depth_forward(field, zf):
    full = dot(field.reshape(YL * C, NZ), zf)
    full = (full[:, :128] + full[:, 128:]).reshape(YL, 4, 8, 128)
    lane = lax.broadcasted_iota(jnp.int32, (YL, 8, 128), 2)
    low = jnp.where(lane < 32, full[:, 0], full[:, 1])
    high = jnp.where(lane < 96, full[:, 2], full[:, 3])
    return jnp.where(lane < 64, low, high)


def put_rows(x, depth, d_ref, rh_ref, rl_ref):
    d_ref[...] = depth.reshape(YL * 8, 128)
    rows = pl.multiple_of(x * 64, 64)
    for c8 in range(8):
        part = d_ref[pl.ds(c8, YL, stride=8), :]
        lanes = slice((c8 % 2) * 128, (c8 % 2) * 128 + 128)
        hi, lo = halves(part)
        rh_ref[c8 // 2, pl.ds(rows, 32), lanes] = hi
        rl_ref[c8 // 2, pl.ds(rows, 32), lanes] = lo
        hi, lo = halves(turn(part))
        rows_t = pl.multiple_of(rows + 32, 32)
        rh_ref[c8 // 2, pl.ds(rows_t, 32), lanes] = hi
        rl_ref[c8 // 2, pl.ds(rows_t, 32), lanes] = lo


class Forward:
    scratch = dict(
        d=pltpu.VMEM((256, 128), F32),
        rh=pltpu.VMEM((4, 512, 256), BF16),
        rl=pltpu.VMEM((4, 512, 256), BF16),
        ys=pltpu.VMEM((4, NARROW, 32, 256), F32),
        yr=pltpu.VMEM((4, NARROW, 32, 256), F32),
        xs=pltpu.VMEM((WIDE, 8, 128), F32),
        xr=pltpu.VMEM((WIDE, 8, 128), F32),
        ms=pltpu.VMEM((WIDE, 1, 128), F32),
        mr=pltpu.VMEM((WIDE, 1, 128), F32),
        y_send=pltpu.SemaphoreType.DMA((4, NARROW)),
        y_recv=pltpu.SemaphoreType.DMA((4, NARROW)),
        x_send=pltpu.SemaphoreType.DMA((WIDE,)),
        x_recv=pltpu.SemaphoreType.DMA((WIDE,)),
        m_send=pltpu.SemaphoreType.DMA((WIDE,)),
        m_recv=pltpu.SemaphoreType.DMA((WIDE,)),
    )

    @staticmethod
    def run(s, n, w, yf_ref, xf_ref):
        def send_y(q, carry):
            out = dot3(yf_ref, None, s.rh[q], s.rl[q])
            s.ys[q] = out.reshape(NARROW, 32, 256)
            s.yr[q, n] = s.ys[q, n]
            others(
                n,
                NARROW,
                lambda t: remote(
                    s.ys.at[q, t], s.yr.at[q, n], s.y_send.at[q, t], s.y_recv.at[q, n], {"narrow": t}
                ).start(),
            )
            return carry

        lax.fori_loop(0, 4, send_y, 0)

        def sum_y(q, carry):
            others(
                n,
                NARROW,
                lambda t: remote(
                    s.ys.at[q, t], s.yr.at[q, t], s.y_send.at[q, t], s.y_recv.at[q, t], {"narrow": t}
                ).wait_recv(),
            )
            total = s.yr[q, 0]
            for t in range(1, NARROW):
                total = total + s.yr[q, t]
            for k in range(KY):
                for j in range(2):
                    to = k * 8 + 2 * q + j
                    tile = total[k * 8 : k * 8 + 8, j * 128 : j * 128 + 128]
                    s.xs[to] = tile

                    @pl.when(to == w)
                    def _():
                        s.xr[w] = s.xs[to]

                    @pl.when(to != w)
                    def _():
                        remote(
                            s.xs.at[to], s.xr.at[w], s.x_send.at[to], s.x_recv.at[w], {"wide": to}
                        ).start()

            return carry

        lax.fori_loop(0, 4, sum_y, 0)
        others(
            w,
            WIDE,
            lambda t: remote(
                s.xs.at[t], s.xr.at[t], s.x_send.at[t], s.x_recv.at[t], {"wide": t}
            ).wait_recv(),
        )
        cells = s.xr[...].reshape(256, 128)
        hi, lo = halves(jnp.concatenate((cells, turn(cells)), axis=0))
        modes = dot3(xf_ref, None, hi, lo)
        s.ms[...] = modes.reshape(WIDE, 1, 128)
        s.mr[w] = s.ms[w]
        others(
            w,
            WIDE,
            lambda t: remote(
                s.ms.at[t], s.mr.at[w], s.m_send.at[t], s.m_recv.at[w], {"wide": t}
            ).start(),
        )
        others(
            w,
            WIDE,
            lambda t: remote(
                s.ms.at[t], s.mr.at[t], s.m_send.at[t], s.m_recv.at[t], {"wide": t}
            ).wait_recv(),
        )

    @staticmethod
    def finish(s, n, w):
        def per_q(q, carry):
            others(
                n,
                NARROW,
                lambda t: remote(
                    s.ys.at[q, t], s.yr.at[q, t], s.y_send.at[q, t], s.y_recv.at[q, t], {"narrow": t}
                ).wait_send(),
            )
            return carry

        lax.fori_loop(0, 4, per_q, 0)

        def per_t(t):
            remote(
                s.xs.at[t], s.xr.at[t], s.x_send.at[t], s.x_recv.at[t], {"wide": t}
            ).wait_send()
            remote(
                s.ms.at[t], s.mr.at[t], s.m_send.at[t], s.m_recv.at[t], {"wide": t}
            ).wait_send()

        others(w, WIDE, per_t)


class Inverse:
    scratch = dict(
        nr=pltpu.VMEM((WIDE, 1, 128), F32),
        vs=pltpu.VMEM((WIDE, 8, 128), F32),
        vr=pltpu.VMEM((KY, 8, 8, 128), F32),
        ag=pltpu.VMEM((KY, NARROW, 8, 8, 128), F32),
        s=pltpu.VMEM((XL * 256, 128), F32),
        n_send=pltpu.SemaphoreType.DMA((WIDE,)),
        n_recv=pltpu.SemaphoreType.DMA((WIDE,)),
        v_send=pltpu.SemaphoreType.DMA((WIDE,)),
        v_recv=pltpu.SemaphoreType.DMA((WIDE,)),
        a_send=pltpu.SemaphoreType.DMA((KY, NARROW)),
        a_recv=pltpu.SemaphoreType.DMA((KY, NARROW)),
    )

    @staticmethod
    def start(s, n, w, modes_ref):
        s.nr[w] = modes_ref[w]
        others(
            w,
            WIDE,
            lambda t: remote(
                modes_ref.at[t], s.nr.at[w], s.n_send.at[t], s.n_recv.at[w], {"wide": t}
            ).start(),
        )

    @staticmethod
    def run(s, n, w, modes_ref, yi_ref, xi_ref):
        others(
            w,
            WIDE,
            lambda t: remote(
                modes_ref.at[t], s.nr.at[t], s.n_send.at[t], s.n_recv.at[t], {"wide": t}
            ).wait_recv(),
        )
        modes = s.nr[...].reshape(WIDE, 128)
        hi, lo = halves(jnp.concatenate((modes, turn(modes)), axis=0))
        cells = dot3(xi_ref, None, hi, lo)
        s.vs[...] = cells.reshape(WIDE, 8, 128)
        own_k, own_c = w // 8, lax.rem(w, 8)
        s.vr[own_k, own_c] = s.vs[w]
        others(
            w,
            WIDE,
            lambda t: remote(
                s.vs.at[t], s.vr.at[own_k, own_c], s.v_send.at[t], s.v_recv.at[w], {"wide": t}
            ).start(),
        )

        def per_k(k, carry):
            def arrived(c, inner):
                t = k * 8 + c

                @pl.when(t != w)
                def _():
                    remote(
                        s.vs.at[t], s.vr.at[k, c], s.v_send.at[t], s.v_recv.at[t], {"wide": t}
                    ).wait_recv()

                return inner

            lax.fori_loop(0, 8, arrived, 0)
            s.ag[k, n] = s.vr[k]
            others(
                n,
                NARROW,
                lambda t: remote(
                    s.vr.at[k], s.ag.at[k, n], s.a_send.at[k, t], s.a_recv.at[k, n], {"narrow": t}
                ).start(),
            )
            return carry

        lax.fori_loop(0, KY, per_k, 0)

    @staticmethod
    def to_depth(s, n, yi_ref):
        def wait_k(k, carry):
            others(
                n,
                NARROW,
                lambda t: remote(
                    s.vr.at[k], s.ag.at[k, t], s.a_send.at[k, t], s.a_recv.at[k, t], {"narrow": t}
                ).wait_recv(),
            )
            return carry

        lax.fori_loop(0, KY, wait_k, 0)

        def pair(p, carry):
            columns = []
            for j in range(2):
                part = s.ag[:, :, 2 * p + j].reshape(256, 128)
                columns.append(jnp.concatenate((part, turn(part)), axis=0))
            hi, lo = halves(jnp.concatenate(columns, axis=1))
            out = dot3(yi_ref, None, hi, lo)
            for x in range(XL):
                for j in range(2):
                    s.s[pl.ds(x * 256 + 2 * p + j, YL, stride=8), :] = out[
                        x * YL : x * YL + YL, j * 128 : j * 128 + 128
                    ]
            return carry

        lax.fori_loop(0, 4, pair, 0)

    @staticmethod
    def depth_inverse(s, x, zi_ref, field_ref):
        rows = pl.multiple_of(x * 256, 256)
        hi, lo = halves(s.s[pl.ds(rows, 256), :])
        both = jnp.concatenate((hi, lo, hi), axis=1)
        for g in range(4):
            field_ref[:, g] = dot(both, zi_ref[g]).reshape(YL, 8, NZ)

    @staticmethod
    def finish(s, n, w, modes_ref):
        def per_t(t):
            remote(
                modes_ref.at[t], s.nr.at[t], s.n_send.at[t], s.n_recv.at[t], {"wide": t}
            ).wait_send()
            remote(
                s.vs.at[t], s.vr.at[0, 0], s.v_send.at[t], s.v_recv.at[t], {"wide": t}
            ).wait_send()

        others(w, WIDE, per_t)

        def per_k(k, carry):
            others(
                n,
                NARROW,
                lambda t: remote(
                    s.vr.at[k], s.ag.at[k, t], s.a_send.at[k, t], s.a_recv.at[k, t], {"narrow": t}
                ).wait_send(),
            )
            return carry

        lax.fori_loop(0, KY, per_k, 0)


class Names:
    def __init__(self, names, refs):
        for name, ref in zip(names, refs):
            setattr(self, name, ref)


def each_x(fn):
    def body(x, carry):
        fn(x)
        return carry

    lax.fori_loop(0, XL, body, 0)


def forward_kernel(names, act_hbm, yf_hbm, xf_ref, zf_ref, out_ref, *refs):
    s = Names(names, refs)
    n, w = lax.axis_index("narrow"), lax.axis_index("wide")
    each_x(lambda x: pltpu.make_async_copy(act_hbm.at[x], s.act.at[x], s.act_sem.at[x]).start())
    table = pltpu.make_async_copy(yf_hbm.at[n], s.yf, s.table_sem.at[0])
    table.start()
    barrier = greet(n, w)

    def step(x):
        pltpu.make_async_copy(act_hbm.at[x], s.act.at[x], s.act_sem.at[x]).wait()
        put_rows(x, depth_forward(s.act[x], zf_ref[...]), s.d, s.rh, s.rl)

    each_x(step)
    table.wait()
    greeted(barrier)
    Forward.run(s, n, w, s.yf, xf_ref)
    out_ref[...] = s.mr[...]
    Forward.finish(s, n, w)


def fold_point(full):
    row = lax.broadcasted_iota(jnp.int32, full.shape, 0) // 32
    lane = lax.broadcasted_iota(jnp.int32, full.shape, 1) // 32
    full = jnp.where(row == lane, full, 0.0)
    total = full[0:32]
    for y in range(1, 8):
        total = total + full[y * 32 : y * 32 + 32]
    total = total[:, :128] + total[:, 128:]
    total = total + pltpu.roll(total, 64, 1)
    total = total + pltpu.roll(total, 32, 1)
    lane = lax.broadcasted_iota(jnp.int32, (8, 128), 1)
    low = jnp.where(lane < 32, total[0:8], total[8:16])
    high = jnp.where(lane < 96, total[16:24], total[24:32])
    return jnp.where(lane < 64, low, high)


def gelu_slope(u):
    k = math.sqrt(2.0 / math.pi)
    square = u * u
    t = jnp.tanh(k * (u + 0.044715 * (square * u)))
    inner = k * (1.0 + (3 * 0.044715) * square)
    return 0.5 * (1.0 + t) + 0.5 * u * ((1.0 - t * t) * inner)


def middle_kernel(
    names,
    modes_ref,
    act_hbm,
    cot_hbm,
    yf_hbm,
    yi_hbm,
    xf_ref,
    xi_ref,
    zf_ref,
    zi_ref,
    mix_ref,
    bias_ref,
    grads_ref,
    sums_ref,
    pre_hbm,
    *refs,
):
    s = Names(names, refs)
    n, w = lax.axis_index("narrow"), lax.axis_index("wide")
    barrier = greet(n, w)
    tables_in = [
        pltpu.make_async_copy(yi_hbm.at[n], s.yi, s.table_sem.at[0]),
        pltpu.make_async_copy(yf_hbm.at[n], s.yf, s.table_sem.at[1]),
    ]
    for copy in tables_in:
        copy.start()

    def fetch(x):
        pltpu.make_async_copy(act_hbm.at[x], s.act.at[x], s.act_sem.at[x]).start()
        pltpu.make_async_copy(cot_hbm.at[x], s.cot.at[x], s.cot_sem.at[x]).start()

    each_x(fetch)
    greeted(barrier)
    Inverse.start(s, n, w, modes_ref)
    s.pg[...] = jnp.zeros_like(s.pg)
    s.bs[...] = jnp.zeros_like(s.bs)
    for copy in tables_in:
        copy.wait()
    Inverse.run(s, n, w, modes_ref, s.yi, xi_ref)
    Inverse.to_depth(s, n, s.yi)

    def step(x):
        pltpu.make_async_copy(act_hbm.at[x], s.act.at[x], s.act_sem.at[x]).wait()
        pltpu.make_async_copy(cot_hbm.at[x], s.cot.at[x], s.cot_sem.at[x]).wait()
        Inverse.depth_inverse(s, x, zi_ref, s.field)

        def block(b, carry):
            ys = pl.ds(pl.multiple_of(b * 8, 8), 8)
            act = s.act[x, ys].reshape(256, NZ)
            point = dot(mix_ref[...], act)
            preact = s.field[ys].reshape(256, NZ) + point + bias_ref[...]
            slope = gelu_slope(preact)
            pre = (s.cot[x, ys].reshape(256, NZ).astype(F32) * slope).astype(BF16)
            s.pre[x, ys] = pre.reshape(8, C, NZ)
            s.pg[...] += lax.dot_general(
                act, pre, (((1,), (1,)), ((), ())), preferred_element_type=F32
            )
            return carry

        lax.fori_loop(0, 4, block, 0)
        pltpu.make_async_copy(s.pre.at[x], pre_hbm.at[x], s.pre_sem.at[x]).start()
        depth = depth_forward(s.pre[x], zf_ref[...])
        s.bs[...] += jnp.sum(depth, axis=0)
        put_rows(x, depth, s.d, s.rh, s.rl)

    each_x(step)
    s.ps[0:8] = fold_point(s.pg[...])
    s.ps[8:16] = s.bs[...]
    s.pr[n] = s.ps[...]
    Forward.run(s, n, w, s.yf, xf_ref)

    def sum_copy(t, at):
        return remote(s.ps, s.pr.at[at], s.p_send.at[t], s.p_recv.at[at], {"narrow": t})

    others(n, NARROW, lambda t: sum_copy(t, n).start())
    grads_ref[...] = s.mr[...]
    others(n, NARROW, lambda t: sum_copy(t, t).wait_recv())
    total = s.pr[0]
    for t in range(1, NARROW):
        total = total + s.pr[t]
    sums_ref[...] = total
    others(n, NARROW, lambda t: sum_copy(t, t).wait_send())
    each_x(lambda x: pltpu.make_async_copy(s.pre.at[x], pre_hbm.at[x], s.pre_sem.at[x]).wait())
    Inverse.finish(s, n, w, modes_ref)
    Forward.finish(s, n, w)


def last_kernel(
    names,
    modes_ref,
    sums_ref,
    pre_hbm,
    yi_hbm,
    xi_ref,
    zi_ref,
    mix_ref,
    out_hbm,
    total_ref,
    *refs,
):
    s = Names(names, refs)
    n, w = lax.axis_index("narrow"), lax.axis_index("wide")
    barrier = greet(n, w)
    table = pltpu.make_async_copy(yi_hbm.at[n], s.yi, s.table_sem.at[0])
    table.start()
    each_x(lambda x: pltpu.make_async_copy(pre_hbm.at[x], s.pre.at[x], s.pre_sem.at[x]).start())
    greeted(barrier)
    Inverse.start(s, n, w, modes_ref)
    table.wait()
    Inverse.run(s, n, w, modes_ref, s.yi, xi_ref)

    def sum_copy(t, at):
        return remote(sums_ref, s.pr.at[at], s.p_send.at[t], s.p_recv.at[at], {"wide": t})

    s.pr[w] = sums_ref[...]
    others(w, WIDE, lambda t: sum_copy(t, w).start())
    Inverse.to_depth(s, n, s.yi)

    def step(x):
        pltpu.make_async_copy(pre_hbm.at[x], s.pre.at[x], s.pre_sem.at[x]).wait()
        Inverse.depth_inverse(s, x, zi_ref, s.field)

        def block(b, carry):
            ys = pl.ds(pl.multiple_of(b * 8, 8), 8)
            point = dot(mix_ref[...], s.pre[x, ys].reshape(256, NZ))
            out = s.field[ys].reshape(256, NZ) + point
            s.out[x, ys] = out.astype(BF16).reshape(8, C, NZ)
            return carry

        lax.fori_loop(0, 4, block, 0)
        pltpu.make_async_copy(s.out.at[x], out_hbm.at[x], s.out_sem.at[x]).start()

    each_x(step)
    others(w, WIDE, lambda t: sum_copy(t, t).wait_recv())
    total = s.pr[0]
    for t in range(1, WIDE):
        total = total + s.pr[t]
    total_ref[...] = total
    others(w, WIDE, lambda t: sum_copy(t, t).wait_send())
    Inverse.finish(s, n, w, modes_ref)
    each_x(lambda x: pltpu.make_async_copy(s.out.at[x], out_hbm.at[x], s.out_sem.at[x]).wait())


VM = pl.BlockSpec(memory_space=pltpu.VMEM)
HB = pl.BlockSpec(memory_space=pl.ANY)


def call(kernel, name, cid, scratch, in_specs, out_specs, out_shape, *operands):
    return pl.pallas_call(
        functools.partial(kernel, tuple(scratch)),
        name=name,
        in_specs=in_specs,
        out_specs=out_specs,
        out_shape=out_shape,
        scratch_shapes=tuple(scratch.values()),
        compiler_params=pltpu.CompilerParams(
            collective_id=cid, has_side_effects=True, vmem_limit_bytes=56 * 1024 * 1024
        ),
    )(*operands)


FIELD = (XL, YL, C, NZ)


def forward_call(act, tabs):
    scratch = dict(
        Forward.scratch,
        act=pltpu.VMEM(FIELD, BF16),
        yf=pltpu.VMEM((2, 256, 512), BF16),
        act_sem=pltpu.SemaphoreType.DMA((XL,)),
        table_sem=pltpu.SemaphoreType.DMA((2,)),
    )
    return call(
        forward_kernel,
        "field_to_modes",
        0,
        scratch,
        [HB, HB, VM, VM],
        VM,
        jax.ShapeDtypeStruct((WIDE, 1, 128), F32),
        act,
        tabs["yf"],
        tabs["xf"],
        tabs["zf"],
    )


def middle_call(modes, act, cot, mix, bias, tabs):
    scratch = dict(
        Forward.scratch,
        **Inverse.scratch,
        act=pltpu.VMEM(FIELD, BF16),
        cot=pltpu.VMEM(FIELD, BF16),
        pre=pltpu.VMEM(FIELD, BF16),
        field=pltpu.VMEM((YL, 4, 8, NZ), F32),
        yf=pltpu.VMEM((2, 256, 512), BF16),
        yi=pltpu.VMEM((2, 256, 512), BF16),
        pg=pltpu.VMEM((256, 256), F32),
        bs=pltpu.VMEM((8, 128), F32),
        ps=pltpu.VMEM((16, 128), F32),
        pr=pltpu.VMEM((NARROW, 16, 128), F32),
        act_sem=pltpu.SemaphoreType.DMA((XL,)),
        cot_sem=pltpu.SemaphoreType.DMA((XL,)),
        pre_sem=pltpu.SemaphoreType.DMA((XL,)),
        table_sem=pltpu.SemaphoreType.DMA((2,)),
        p_send=pltpu.SemaphoreType.DMA((NARROW,)),
        p_recv=pltpu.SemaphoreType.DMA((NARROW,)),
    )
    return call(
        middle_kernel,
        "modes_to_gradient_modes",
        1,
        scratch,
        [VM, HB, HB, HB, HB, VM, VM, VM, VM, VM, VM],
        [VM, VM, HB],
        [
            jax.ShapeDtypeStruct((WIDE, 1, 128), F32),
            jax.ShapeDtypeStruct((16, 128), F32),
            jax.ShapeDtypeStruct(FIELD, BF16),
        ],
        modes,
        act,
        cot,
        tabs["yf"],
        tabs["yi"],
        tabs["xf"],
        tabs["xi"],
        tabs["zf"],
        tabs["ziw"],
        mix,
        bias,
    )


def last_call(modes, sums, pre, mix, tabs):
    scratch = dict(
        Inverse.scratch,
        pre=pltpu.VMEM(FIELD, BF16),
        out=pltpu.VMEM(FIELD, BF16),
        field=pltpu.VMEM((YL, 4, 8, NZ), F32),
        yi=pltpu.VMEM((2, 256, 512), BF16),
        pr=pltpu.VMEM((WIDE, 16, 128), F32),
        pre_sem=pltpu.SemaphoreType.DMA((XL,)),
        out_sem=pltpu.SemaphoreType.DMA((XL,)),
        table_sem=pltpu.SemaphoreType.DMA((2,)),
        p_send=pltpu.SemaphoreType.DMA((WIDE,)),
        p_recv=pltpu.SemaphoreType.DMA((WIDE,)),
    )
    return call(
        last_kernel,
        "modes_to_input_gradient",
        2,
        scratch,
        [VM, VM, HB, HB, VM, VM, VM],
        [HB, VM],
        [jax.ShapeDtypeStruct(FIELD, BF16), jax.ShapeDtypeStruct((16, 128), F32)],
        modes,
        sums,
        pre,
        tabs["yi"],
        tabs["xi"],
        tabs["zi1"],
        mix,
    )


def precise(form, left, right):
    return jnp.einsum(form, left, right, precision=lax.Precision.HIGHEST, preferred_element_type=F32)


def modes_in(rows):
    return rows.reshape(KY, 8, 4, 2, M).transpose(3, 0, 4, 2, 1).reshape(2, KY, M, C)


def modes_out(parts):
    return (
        parts.reshape(2, KY, M, 4, 8).transpose(1, 4, 3, 0, 2).reshape(WIDE, 1, 128)
    )


def local(activations, cotangent, point_weight, bias, spectral_weight):
    tabs = {name: jnp.asarray(value) for name, value in tables().items()}
    eye = jnp.eye(8, dtype=BF16)
    mix = jnp.kron(eye, point_weight.T)
    mix_back = jnp.kron(eye, point_weight)
    bias_rows = jnp.tile(bias, 8)[:, None]
    weight = spectral_weight[:, 0].astype(F32)

    coeffs = modes_in(forward_call(activations, tabs))
    ahead = "qkc,qkco->qko"
    mixed = jnp.stack(
        (
            precise(ahead, coeffs[0], weight[0]) - precise(ahead, coeffs[1], weight[1]),
            precise(ahead, coeffs[0], weight[1]) + precise(ahead, coeffs[1], weight[0]),
        )
    )
    grad_rows, sums, pre = middle_call(
        modes_out(mixed), activations, cotangent, mix, bias_rows, tabs
    )
    depth_weights = jnp.where(jnp.arange(M, dtype=jnp.int32) == 0, 1.0, 2.0).astype(F32)
    grads = modes_in(grad_rows) * depth_weights[None, None, :, None]
    cr, ci = coeffs[0][..., :, None], coeffs[1][..., :, None]
    gr, gi = grads[0][..., None, :], grads[1][..., None, :]
    spectral_grad = jnp.stack((cr * gr + ci * gi, cr * gi - ci * gr))[:, None]
    back = "qko,qkco->qkc"
    coeff_grad = jnp.stack(
        (
            precise(back, grads[0], weight[0]) + precise(back, grads[1], weight[1]),
            precise(back, grads[1], weight[0]) - precise(back, grads[0], weight[1]),
        )
    )
    input_grad, total = last_call(modes_out(coeff_grad), sums, pre, mix_back, tabs)
    point_grad = total[0:8].reshape(8, 4, C).transpose(1, 0, 2).reshape(C, C) * SCALE
    bias_grad = total[8:16].reshape(8, 4, 2, M)[:, :, 0, 0].T.reshape(C) * SCALE
    return (input_grad, point_grad, bias_grad, spectral_grad)


def solution(mesh):
    return jax.shard_map(
        local,
        mesh=mesh,
        in_specs=(
            P("wide", "narrow", None, None),
            P("wide", "narrow", None, None),
            P(),
            P(),
            P(None, "wide", "narrow", None, None, None),
        ),
        out_specs=(
            P("wide", "narrow", None, None),
            P(),
            P(),
            P(None, "wide", "narrow", None, None, None),
        ),
        check_vma=False,
    )
```

```python
import functools
import math

import jax
import jax.numpy as jnp
import ml_dtypes
import numpy as np
from jax import lax
from jax.experimental import pallas as pl
from jax.experimental.pallas import tpu as pltpu
from jax.sharding import PartitionSpec as P

WIDE = 32
NARROW = 8
M = 16
C = 32
NZ = 256
XL = 8
YL = 32
KY = 4
XC = 2
CHUNKS = XL // XC
ROWS = KY * XC
SCALE = 1.0 / 4096.0

F32 = jnp.float32
BF16 = jnp.bfloat16


def kept(j):
    return np.where(j < 16, j, 224 + j)


def trig(freqs, cells):
    angle = (np.outer(freqs, cells) % 256) * (2.0 * math.pi / 256.0)
    return np.cos(angle), np.sin(angle)


def split_np(table):
    hi = table.astype(np.float32).astype(ml_dtypes.bfloat16)
    lo = (table - hi.astype(np.float64)).astype(np.float32).astype(ml_dtypes.bfloat16)
    return hi, lo


@functools.lru_cache(maxsize=None)
def tables():
    freqs = kept(np.arange(32))
    cos_a, sin_a = trig(freqs, np.arange(256))
    cos_z, sin_z = trig(np.arange(M), np.arange(NZ))
    eye_x = np.eye(XC)
    cy = cos_a.reshape(NARROW, KY, NARROW, YL)
    sy = sin_a.reshape(NARROW, KY, NARROW, YL)
    both = np.stack((cy, sy))
    yf = np.einsum("dtkny,xu->ntkxudy", both, eye_x).reshape(NARROW, 32 * XC, 64 * XC)
    both = np.stack((cy, -sy))
    yi = np.einsum("dtkny,xu->nxydtku", both, eye_x).reshape(NARROW, 32 * XC, 64 * XC)
    xf = np.concatenate((cos_a, sin_a), axis=1) * SCALE
    xi = np.concatenate((cos_a.T, -sin_a.T), axis=1)
    zf = np.tile(np.concatenate((cos_z, -sin_z), axis=0).T, (1, 4))
    depth = np.where(np.arange(M) == 0, 1.0, 2.0)[:, None]

    def inverse_z(weights):
        one = np.concatenate((cos_z * weights, -sin_z * weights), axis=0) * SCALE
        full = np.zeros((4, 128, NZ))
        for g in range(4):
            full[g, g * 32 : (g + 1) * 32] = one
        hi, lo = split_np(full)
        return np.concatenate((hi, hi, lo), axis=1)

    return dict(
        yf=np.stack(split_np(yf), axis=1),
        yi=np.stack(split_np(yi), axis=1),
        xf=np.stack(split_np(xf)),
        xi=np.stack(split_np(xi)),
        zf=np.concatenate(split_np(zf), axis=1),
        ziw=inverse_z(depth),
        zi1=inverse_z(np.ones((M, 1))),
    )


def dot(a, b):
    return jnp.dot(a, b, preferred_element_type=F32)


def dot_t(a, b):
    return lax.dot_general(a, b, (((1,), (1,)), ((), ())), preferred_element_type=F32)


def halves(x):
    hi = x.astype(BF16)
    return hi, (x - hi.astype(F32)).astype(BF16)


def dot3(table, hi, lo):
    t_hi, t_lo = table[0], table[1]
    return dot(t_hi, hi) + (dot(t_hi, lo) + dot(t_lo, hi))


def lane_of(shape):
    return lax.broadcasted_iota(jnp.int32, shape, len(shape) - 1)


def turn(x):
    real = lax.rem(lane_of(x.shape), 32) < 16
    return jnp.where(real, pltpu.roll(x, 112, x.ndim - 1), -pltpu.roll(x, 16, x.ndim - 1))


def remote(src, dst, send, recv, device):
    return pltpu.make_async_remote_copy(
        src_ref=src,
        dst_ref=dst,
        send_sem=send,
        recv_sem=recv,
        device_id=device,
        device_id_type=pl.DeviceIdType.MESH,
    )


def others(me, size, fn):
    def body(k, carry):
        fn(lax.rem(me + k, size))
        return carry

    lax.fori_loop(1, size, body, 0)


def greet(n, w):
    barrier = pltpu.get_barrier_semaphore()

    def signal(axis):
        return lambda t: pl.semaphore_signal(
            barrier, inc=1, device_id={axis: t}, device_id_type=pl.DeviceIdType.MESH
        )

    others(n, NARROW, signal("narrow"))
    others(w, WIDE, signal("wide"))
    return barrier


def greeted(barrier):
    pl.semaphore_wait(barrier, NARROW + WIDE - 2)


def loop(count, fn):
    def body(i, carry):
        fn(i)
        return carry

    lax.fori_loop(0, count, body, 0)


class Names:
    def __init__(self, names, refs):
        for name, ref in zip(names, refs):
            setattr(self, name, ref)


class Round:
    def __init__(self, axis, size, me, src, dst, send, recv):
        self.axis, self.size, self.me = axis, size, me
        self.src, self.dst, self.send, self.recv = src, dst, send, recv

    def start(self, whole=False):
        def one(t):
            remote(
                self.src if whole else self.src.at[t],
                self.dst.at[self.me],
                self.send,
                self.recv,
                {self.axis: t},
            ).start()

        others(self.me, self.size, one)

    def all_of(self):
        part = self.dst.at[pl.ds(0, self.size - 1)]
        return remote(part, part, self.send, self.recv, {self.axis: lax.rem(self.me + 1, self.size)})

    def arrived(self):
        self.all_of().wait_recv()

    def sent(self):
        self.all_of().wait_send()


FORWARD = dict(
    ys=pltpu.VMEM((CHUNKS, NARROW, ROWS, 1024), F32),
    yr=pltpu.VMEM((CHUNKS, NARROW, ROWS, 1024), F32),
    xs=pltpu.VMEM((WIDE, 8, 128), F32),
    xr=pltpu.VMEM((WIDE, 8, 128), F32),
    ms=pltpu.VMEM((WIDE, 1, 128), F32),
    mr=pltpu.VMEM((WIDE, 1, 128), F32),
    ysem=pltpu.SemaphoreType.DMA((2, CHUNKS)),
    xsem=pltpu.SemaphoreType.DMA((2,)),
    msem=pltpu.SemaphoreType.DMA((2,)),
)

INVERSE = dict(
    ns=pltpu.VMEM((WIDE, 1, 128), F32),
    nr=pltpu.VMEM((WIDE, 1, 128), F32),
    vs=pltpu.VMEM((WIDE, 8, 128), F32),
    vr=pltpu.VMEM((WIDE, 8, 128), F32),
    as_=pltpu.VMEM((CHUNKS, ROWS, 1024), F32),
    ar=pltpu.VMEM((CHUNKS, NARROW, ROWS, 1024), F32),
    nsem=pltpu.SemaphoreType.DMA((2,)),
    vsem=pltpu.SemaphoreType.DMA((2,)),
    asem=pltpu.SemaphoreType.DMA((2, CHUNKS)),
)


def depth_forward(field, zf):
    full = dot(field.reshape(YL * C, NZ), zf)
    full = (full[:, :128] + full[:, 128:]).reshape(YL, 4, 8, 128)
    lane = lane_of((YL, 8, 128))
    low = jnp.where(lane < 32, full[:, 0], full[:, 1])
    high = jnp.where(lane < 96, full[:, 2], full[:, 3])
    return jnp.where(lane < 64, low, high)


class Forward:
    def __init__(self, s, own, n, w):
        self.s, self.own, self.n, self.w = s, own, n, w
        self.x = Round("wide", WIDE, w, own.xs, own.xr, own.xsem.at[0], own.xsem.at[1])
        self.m = Round("wide", WIDE, w, own.ms, own.mr, own.msem.at[0], own.msem.at[1])

    def y(self, q):
        o = self.own
        return Round("narrow", NARROW, self.n, o.ys.at[q], o.yr.at[q], o.ysem.at[0, q], o.ysem.at[1, q])

    def put_rows(self, i, depth):
        s = self.s
        s.d[...] = depth.reshape(YL * 8, 128)
        rows = pl.multiple_of(i * 64, 64)
        turned = pl.multiple_of(i * 64 + 32, 32)
        for c8 in range(8):
            part = s.d[pl.ds(c8, YL, stride=8), :]
            lanes = slice(c8 * 128, c8 * 128 + 128)
            s.rh[pl.ds(rows, 32), lanes], s.rl[pl.ds(rows, 32), lanes] = halves(part)
            s.rh[pl.ds(turned, 32), lanes], s.rl[pl.ds(turned, 32), lanes] = halves(turn(part))

    def send_chunk(self, q):
        s, o = self.s, self.own
        out = dot3(s.yf, s.rh[...], s.rl[...])
        o.ys[q] = out.reshape(NARROW, ROWS, 1024)
        o.yr[q, self.n] = o.ys[q, self.n]
        self.y(q).start()

    def sum_chunks(self):
        o = self.own
        for q in range(CHUNKS):
            self.y(q).arrived()
            total = o.yr[q, 0]
            for t in range(1, NARROW):
                total = total + o.yr[q, t]
            for k in range(KY):
                for c8 in range(8):
                    o.xs[k * 8 + c8, q * XC : q * XC + XC] = total[
                        k * XC : k * XC + XC, c8 * 128 : c8 * 128 + 128
                    ]
        o.xr[self.w] = o.xs[self.w]
        self.x.start()

    def to_owner(self, xf):
        o = self.own
        self.x.arrived()
        cells = o.xr[...].reshape(256, 128)
        hi, lo = halves(jnp.concatenate((cells, turn(cells)), axis=0))
        o.ms[...] = dot3(xf, hi, lo).reshape(WIDE, 1, 128)
        o.mr[self.w] = o.ms[self.w]
        self.m.start()

    def modes(self):
        self.m.arrived()
        return self.own.mr[...].reshape(WIDE, 128)

    def finish(self):
        loop(CHUNKS, lambda q: self.y(q).sent())
        self.x.sent()
        self.m.sent()


class Inverse:
    def __init__(self, s, own, n, w):
        self.s, self.own, self.n, self.w = s, own, n, w
        self.m = Round("wide", WIDE, w, own.ns, own.nr, own.nsem.at[0], own.nsem.at[1])
        self.x = Round("wide", WIDE, w, own.vs, own.vr, own.vsem.at[0], own.vsem.at[1])

    def y(self, q):
        o = self.own
        return Round("narrow", NARROW, self.n, o.as_.at[q], o.ar.at[q], o.asem.at[0, q], o.asem.at[1, q])

    def start(self, modes):
        o = self.own
        o.ns[...] = modes.reshape(WIDE, 1, 128)
        o.nr[self.w] = o.ns[self.w]
        self.m.start()

    def to_cells(self, xi):
        o = self.own
        self.m.arrived()
        modes = o.nr[...].reshape(WIDE, 128)
        hi, lo = halves(jnp.concatenate((modes, turn(modes)), axis=0))
        o.vs[...] = dot3(xi, hi, lo).reshape(WIDE, 8, 128)
        o.vr[self.w] = o.vs[self.w]
        self.x.start()

    def gather(self):
        o = self.own
        self.x.arrived()
        for q in range(CHUNKS):
            for k in range(KY):
                for c8 in range(8):
                    o.as_[q, k * XC : k * XC + XC, c8 * 128 : c8 * 128 + 128] = o.vr[
                        k * 8 + c8, q * XC : q * XC + XC
                    ]
            o.ar[q, self.n] = o.as_[q]
            self.y(q).start(whole=True)

    def chunk(self, q):
        s, o = self.s, self.own
        self.y(q).arrived()
        columns = []
        for c8 in range(8):
            part = o.ar[q, :, :, c8 * 128 : c8 * 128 + 128].reshape(NARROW * ROWS, 128)
            columns.append(jnp.concatenate((part, turn(part)), axis=0))
        hi, lo = halves(jnp.concatenate(columns, axis=1))
        out = dot3(s.yi, hi, lo)
        for i in range(XC):
            for c8 in range(8):
                s.s[pl.ds(i * 256 + c8, YL, stride=8), :] = out[
                    i * YL : i * YL + YL, c8 * 128 : c8 * 128 + 128
                ]

    def field_row(self, i, zi):
        s = self.s
        hi, lo = halves(s.s[pl.ds(pl.multiple_of(i * 256, 256), 256), :])
        both = jnp.concatenate((hi, lo, hi), axis=1)
        for g in range(4):
            s.field[:, g] = dot(both, zi[g]).reshape(YL, 8, NZ)

    def finish(self):
        self.m.sent()
        self.x.sent()
        loop(CHUNKS, lambda q: self.y(q).sent())


def fold_point(full):
    row = lax.broadcasted_iota(jnp.int32, full.shape, 0) // 32
    full = jnp.where(row == lane_of(full.shape) // 32, full, 0.0)
    total = full[0:32]
    for y in range(1, 8):
        total = total + full[y * 32 : y * 32 + 32]
    total = total[:, :128] + total[:, 128:]
    total = total + pltpu.roll(total, 64, 1)
    total = total + pltpu.roll(total, 32, 1)
    lane = lane_of((8, 128))
    low = jnp.where(lane < 32, total[0:8], total[8:16])
    high = jnp.where(lane < 96, total[16:24], total[24:32])
    return jnp.where(lane < 64, low, high)


def gelu_slope(u):
    k = math.sqrt(2.0 / math.pi)
    square = u * u
    h = 0.5 * jnp.tanh(u * (k + (k * 0.044715) * square)) + 0.5
    return h + h * (1.0 - h) * (u * (2.0 * k + (6.0 * k * 0.044715) * square))


def spread(rows, j):
    return group_sum(jnp.where(lane_of(rows.shape) // 16 == j, rows, 0.0))


def group_sum(v):
    v = v + pltpu.roll(v, 64, 1)
    v = v + pltpu.roll(v, 32, 1)
    return v + pltpu.roll(v, 16, 1)


def mix_modes(s, modes, weight_ref):
    for j in range(8):
        s.rep[j] = spread(modes, j)

    def body(c8, carry):
        first, second = carry
        for g in range(4):
            weight = weight_ref[c8 * 4 + g].astype(F32)

            def rows(part):
                return jnp.concatenate(
                    [
                        jnp.broadcast_to(s.rep[2 * g + part, pl.ds(k * 8 + c8, 1), :], (8, 128))
                        for k in range(KY)
                    ],
                    axis=0,
                )

            first = first + rows(0) * weight
            second = second + rows(1) * weight
        return first, second

    zero = jnp.zeros((WIDE, 128), F32)
    first, second = lax.fori_loop(0, 8, body, (zero, zero))
    return first - turn(second)


def mix_back(s, grads, weight_ref):
    turned = turn(grads)

    def body(c8):
        for g in range(4):
            weight = weight_ref[c8 * 4 + g].astype(F32)
            for part, field in enumerate((grads, turned)):
                total = jnp.sum((field * weight).reshape(KY, 8, 128), axis=1)
                for k in range(KY):
                    s.back[2 * g + part, k, pl.ds(c8, 1), :] = total[k : k + 1]

    loop(8, body)
    out = jnp.zeros((WIDE, 128), F32)
    for j in range(8):
        whole = group_sum(s.back[j].reshape(WIDE, 128))
        out = jnp.where(lane_of(out.shape) // 16 == j, whole, out)
    return out


def kernel(
    names,
    act_hbm,
    cot_hbm,
    point_ref,
    bias_ref,
    weight_ref,
    yf_hbm,
    yi_hbm,
    xf_ref,
    xi_ref,
    zf_ref,
    ziw_ref,
    zi1_ref,
    out_hbm,
    total_ref,
    coeffs_ref,
    grads_ref,
    *refs,
):
    s = Names(names, refs)
    n, w = lax.axis_index("narrow"), lax.axis_index("wide")

    def group(prefix, keys):
        keys = tuple(keys)
        return Names(keys, [getattr(s, prefix + key) for key in keys])

    ahead = Forward(s, group("f1_", FORWARD), n, w)
    grad = Forward(s, group("f2_", FORWARD), n, w)
    mixed_in = Inverse(s, group("i1_", INVERSE), n, w)
    back_in = Inverse(s, group("i2_", INVERSE), n, w)

    def act_copy(x):
        return pltpu.make_async_copy(act_hbm.at[x], s.act.at[x], s.act_sem.at[x])

    def cot_copy(x):
        return pltpu.make_async_copy(cot_hbm.at[x], s.cot.at[x], s.cot_sem.at[x])

    def out_copy(x):
        return pltpu.make_async_copy(s.out.at[x], out_hbm.at[x], s.out_sem.at[x])

    table_in = [
        pltpu.make_async_copy(yf_hbm.at[n], s.yf, s.table_sem.at[0]),
        pltpu.make_async_copy(yi_hbm.at[n], s.yi, s.table_sem.at[1]),
    ]
    barrier = greet(n, w)
    loop(XL, lambda x: act_copy(x).start())
    for copy in table_in:
        copy.start()
    loop(XL, lambda x: cot_copy(x).start())
    for copy in table_in:
        copy.wait()

    def forward_chunk(q):
        def row(i):
            x = q * XC + i
            act_copy(x).wait()
            ahead.put_rows(i, depth_forward(s.act[x], zf_ref[...]))

        loop(XC, row)

        @pl.when(q == 0)
        def _():
            greeted(barrier)

        ahead.send_chunk(q)

    loop(CHUNKS, forward_chunk)

    row = lax.broadcasted_iota(jnp.int32, (256, 32), 0)
    pick = lax.rem(row, 32) == lane_of((256, 32))
    ones = jnp.where(pick, 1.0, 0.0).astype(BF16)
    bias_rows = jnp.sum(jnp.where(pick, bias_ref[...], 0.0), axis=1, keepdims=True)
    same = lax.broadcasted_iota(jnp.int32, (256, 256), 0) // 32 == lane_of((256, 256)) // 32
    tall = dot(ones, point_ref[...]).astype(BF16)
    s.mix_back[...] = jnp.where(same, dot_t(tall, ones), 0.0).astype(BF16)
    tall = dot_t(ones, point_ref[...]).astype(BF16)
    s.mix[...] = jnp.where(same, dot_t(tall, ones), 0.0).astype(BF16)

    def blocks(fn):
        def one(i):
            fn(i // 4, pl.ds(pl.multiple_of(lax.rem(i, 4) * 8, 8), 8))

        loop(4 * XL, one)

    def mix_block(x, ys):
        point = dot(s.mix[...], s.act[x, ys].reshape(256, NZ)) + bias_rows
        s.point[x, ys] = point.reshape(8, C, NZ)

    blocks(mix_block)
    ahead.sum_chunks()
    ahead.to_owner(xf_ref)
    coeffs = ahead.modes()
    mixed_in.start(mix_modes(s, coeffs, weight_ref))
    coeffs_ref[...] = ahead.own.mr[...]
    s.bs[...] = jnp.zeros_like(s.bs)
    s.pg[...] = jnp.zeros_like(s.pg)
    mixed_in.to_cells(xi_ref)
    mixed_in.gather()

    def middle_chunk(q):
        mixed_in.chunk(q)

        def row(i):
            x = q * XC + i
            cot_copy(x).wait()
            mixed_in.field_row(i, ziw_ref)

            def block(b):
                ys = pl.ds(pl.multiple_of(b * 8, 8), 8)
                preact = s.field[ys].reshape(256, NZ) + s.point[x, ys].reshape(256, NZ)
                cot = s.cot[x, ys].reshape(256, NZ).astype(F32)
                pre = (cot * gelu_slope(preact)).astype(BF16)
                s.pre[x, ys] = pre.reshape(8, C, NZ)

            loop(4, block)
            depth = depth_forward(s.pre[x], zf_ref[...])
            s.bs[...] += jnp.sum(depth, axis=0)
            grad.put_rows(i, depth)

        loop(XC, row)
        grad.send_chunk(q)

    loop(CHUNKS, middle_chunk)

    def back_block(x, ys):
        pre = s.pre[x, ys].reshape(256, NZ)
        s.pg[...] += dot_t(s.act[x, ys].reshape(256, NZ), pre)
        s.point[x, ys] = dot(s.mix_back[...], pre).reshape(8, C, NZ)

    blocks(back_block)
    s.ps[0:8] = fold_point(s.pg[...])
    s.ps[8:16] = s.bs[...]
    s.pr[n] = s.ps[...]
    grad.sum_chunks()
    narrow_sum = Round("narrow", NARROW, n, s.ps, s.pr, s.psem.at[0], s.psem.at[1])
    narrow_sum.start(whole=True)
    grad.to_owner(xf_ref)
    narrow_sum.arrived()
    total = s.pr[0]
    for t in range(1, NARROW):
        total = total + s.pr[t]
    s.ts[...] = total
    s.tr[w] = total
    rows = grad.modes()
    depth_weight = jnp.where(lax.rem(lane_of(rows.shape), 16) == 0, 1.0, 2.0)
    grads = rows * depth_weight
    back_in.start(mix_back(s, grads, weight_ref))
    grads_ref[...] = grads.reshape(WIDE, 1, 128)
    back_in.to_cells(xi_ref)
    wide_sum = Round("wide", WIDE, w, s.ts, s.tr, s.tsem.at[0], s.tsem.at[1])
    back_in.gather()
    wide_sum.start(whole=True)

    def last_chunk(q):
        back_in.chunk(q)

        def row(i):
            x = q * XC + i
            back_in.field_row(i, zi1_ref)

            def block(b):
                ys = pl.ds(pl.multiple_of(b * 8, 8), 8)
                out = s.field[ys].reshape(256, NZ) + s.point[x, ys].reshape(256, NZ)
                s.out[x, ys] = out.astype(BF16).reshape(8, C, NZ)

            loop(4, block)
            out_copy(x).start()

        loop(XC, row)

    loop(CHUNKS, last_chunk)
    wide_sum.arrived()
    total = s.tr[0]
    for t in range(1, WIDE):
        total = total + s.tr[t]
    total_ref[...] = total
    for part in (ahead, grad, mixed_in, back_in):
        part.finish()
    narrow_sum.sent()
    wide_sum.sent()
    loop(XL, lambda x: out_copy(x).wait())


VM = pl.BlockSpec(memory_space=pltpu.VMEM)
HB = pl.BlockSpec(memory_space=pl.ANY)
FIELD = (XL, YL, C, NZ)


def local(activations, cotangent, point_weight, bias, spectral_weight):
    tabs = {name: jnp.asarray(value) for name, value in tables().items()}
    weight = (
        spectral_weight.reshape(2, KY, M, 4, 8, 4, 8)
        .transpose(4, 3, 1, 6, 5, 0, 2)
        .reshape(C, WIDE, 128)
    )
    scratch = dict(
        act=pltpu.VMEM(FIELD, BF16),
        cot=pltpu.VMEM(FIELD, BF16),
        pre=pltpu.VMEM(FIELD, BF16),
        out=pltpu.VMEM(FIELD, BF16),
        point=pltpu.VMEM(FIELD, F32),
        field=pltpu.VMEM((YL, 4, 8, NZ), F32),
        d=pltpu.VMEM((256, 128), F32),
        rh=pltpu.VMEM((64 * XC, 1024), BF16),
        rl=pltpu.VMEM((64 * XC, 1024), BF16),
        s=pltpu.VMEM((XC * 256, 128), F32),
        yf=pltpu.VMEM((2, 32 * XC, 64 * XC), BF16),
        yi=pltpu.VMEM((2, 32 * XC, 64 * XC), BF16),
        mix=pltpu.VMEM((256, 256), BF16),
        mix_back=pltpu.VMEM((256, 256), BF16),
        rep=pltpu.VMEM((8, WIDE, 128), F32),
        back=pltpu.VMEM((8, KY, 8, 128), F32),
        pg=pltpu.VMEM((256, 256), F32),
        bs=pltpu.VMEM((8, 128), F32),
        ps=pltpu.VMEM((16, 128), F32),
        pr=pltpu.VMEM((NARROW, 16, 128), F32),
        ts=pltpu.VMEM((16, 128), F32),
        tr=pltpu.VMEM((WIDE, 16, 128), F32),
        act_sem=pltpu.SemaphoreType.DMA((XL,)),
        cot_sem=pltpu.SemaphoreType.DMA((XL,)),
        out_sem=pltpu.SemaphoreType.DMA((XL,)),
        table_sem=pltpu.SemaphoreType.DMA((2,)),
        psem=pltpu.SemaphoreType.DMA((2,)),
        tsem=pltpu.SemaphoreType.DMA((2,)),
    )
    for prefix, group in (("f1_", FORWARD), ("f2_", FORWARD), ("i1_", INVERSE), ("i2_", INVERSE)):
        scratch.update({prefix + key: value for key, value in group.items()})
    input_grad, total, coeffs, grads = pl.pallas_call(
        functools.partial(kernel, tuple(scratch)),
        name="layer_backward",
        in_specs=[HB, HB, VM, VM, VM, HB, HB, VM, VM, VM, VM, VM],
        out_specs=[HB, VM, VM, VM],
        out_shape=[
            jax.ShapeDtypeStruct(FIELD, BF16),
            jax.ShapeDtypeStruct((16, 128), F32),
            jax.ShapeDtypeStruct((WIDE, 1, 128), F32),
            jax.ShapeDtypeStruct((WIDE, 1, 128), F32),
        ],
        scratch_shapes=tuple(scratch.values()),
        compiler_params=pltpu.CompilerParams(
            collective_id=0, has_side_effects=True, vmem_limit_bytes=56 * 1024 * 1024
        ),
    )(
        activations,
        cotangent,
        point_weight,
        bias[None],
        weight,
        *(tabs[name] for name in ("yf", "yi", "xf", "xi", "zf", "ziw", "zi1")),
    )

    def modes_in(rows):
        return rows.reshape(KY, 8, 4, 2, M).transpose(3, 0, 4, 2, 1).reshape(2, KY, M, C)

    coeffs, grads = modes_in(coeffs), modes_in(grads)
    cr, ci = coeffs[0][..., :, None], coeffs[1][..., :, None]
    gr, gi = grads[0][..., None, :], grads[1][..., None, :]
    spectral_grad = jnp.stack((cr * gr + ci * gi, cr * gi - ci * gr))[:, None]
    point_grad = total[0:8].reshape(8, 4, C).transpose(1, 0, 2).reshape(C, C) * SCALE
    bias_grad = total[8:16].reshape(8, 4, 2, M)[:, :, 0, 0].T.reshape(C) * SCALE
    return (input_grad, point_grad, bias_grad, spectral_grad)


def solution(mesh):
    return jax.shard_map(
        local,
        mesh=mesh,
        in_specs=(
            P("wide", "narrow", None, None),
            P("wide", "narrow", None, None),
            P(),
            P(),
            P(None, "wide", "narrow", None, None, None),
        ),
        out_specs=(
            P("wide", "narrow", None, None),
            P(),
            P(),
            P(None, "wide", "narrow", None, None, None),
        ),
        check_vma=False,
    )
```

```python
import functools
import math

import jax
import jax.numpy as jnp
import ml_dtypes
import numpy as np
from jax import lax
from jax.experimental import pallas as pl
from jax.experimental.pallas import tpu as pltpu
from jax.sharding import PartitionSpec as P

WIDE = 32
NARROW = 8
M = 16
C = 32
NZ = 256
XL = 8
YL = 32
KY = 4
XC = 2
CHUNKS = XL // XC
ROWS = KY * XC
SCALE = 1.0 / 4096.0

F32 = jnp.float32
BF16 = jnp.bfloat16


def kept(j):
    return np.where(j < 16, j, 224 + j)


def trig(freqs, cells):
    angle = (np.outer(freqs, cells) % 256) * (2.0 * math.pi / 256.0)
    return np.cos(angle), np.sin(angle)


def split_np(table):
    hi = table.astype(np.float32).astype(ml_dtypes.bfloat16)
    lo = (table - hi.astype(np.float64)).astype(np.float32).astype(ml_dtypes.bfloat16)
    return hi, lo


@functools.lru_cache(maxsize=None)
def tables():
    freqs = kept(np.arange(32))
    cos_a, sin_a = trig(freqs, np.arange(256))
    cos_z, sin_z = trig(np.arange(M), np.arange(NZ))
    eye_x = np.eye(XC)
    cy = cos_a.reshape(NARROW, KY, NARROW, YL)
    sy = sin_a.reshape(NARROW, KY, NARROW, YL)
    both = np.stack((cy, sy))
    yf = np.einsum("dtkny,xu->ntkxudy", both, eye_x).reshape(NARROW, 32 * XC, 64 * XC)
    both = np.stack((cy, -sy))
    yi = np.einsum("dtkny,xu->nxydtku", both, eye_x).reshape(NARROW, 32 * XC, 64 * XC)
    xf = np.concatenate((cos_a, sin_a), axis=1) * SCALE
    xi = np.concatenate((cos_a.T, -sin_a.T), axis=1)
    zf = np.tile(np.concatenate((cos_z, -sin_z), axis=0).T, (1, 4))
    depth = np.where(np.arange(M) == 0, 1.0, 2.0)[:, None]

    def inverse_z(weights):
        one = np.concatenate((cos_z * weights, -sin_z * weights), axis=0) * SCALE
        full = np.zeros((4, 128, NZ))
        for g in range(4):
            full[g, g * 32 : (g + 1) * 32] = one
        hi, lo = split_np(full)
        return np.concatenate((hi, hi, lo), axis=1)

    return dict(
        yf=np.stack(split_np(yf), axis=1),
        yi=np.stack(split_np(yi), axis=1),
        xf=np.stack(split_np(xf)),
        xi=np.stack(split_np(xi)),
        zf=np.concatenate(split_np(zf), axis=1),
        ziw=inverse_z(depth),
        zi1=inverse_z(np.ones((M, 1))),
    )


def dot(a, b):
    return jnp.dot(a, b, preferred_element_type=F32)


def dot_t(a, b):
    return lax.dot_general(a, b, (((1,), (1,)), ((), ())), preferred_element_type=F32)


def halves(x):
    hi = x.astype(BF16)
    return hi, (x - hi.astype(F32)).astype(BF16)


def dot3(table, hi, lo):
    t_hi, t_lo = table[0], table[1]
    return dot(t_hi, hi) + (dot(t_hi, lo) + dot(t_lo, hi))


def lane_of(shape):
    return lax.broadcasted_iota(jnp.int32, shape, len(shape) - 1)


def turn(x):
    real = lax.rem(lane_of(x.shape), 32) < 16
    return jnp.where(real, pltpu.roll(x, 112, x.ndim - 1), -pltpu.roll(x, 16, x.ndim - 1))


def remote(src, dst, send, recv, device):
    return pltpu.make_async_remote_copy(
        src_ref=src,
        dst_ref=dst,
        send_sem=send,
        recv_sem=recv,
        device_id=device,
        device_id_type=pl.DeviceIdType.MESH,
    )


def others(me, size, fn):
    def body(k, carry):
        fn(lax.rem(me + k, size))
        return carry

    lax.fori_loop(1, size, body, 0)


def greet(n, w):
    barrier = pltpu.get_barrier_semaphore()

    def signal(axis):
        return lambda t: pl.semaphore_signal(
            barrier, inc=1, device_id={axis: t}, device_id_type=pl.DeviceIdType.MESH
        )

    others(n, NARROW, signal("narrow"))
    others(w, WIDE, signal("wide"))
    return barrier


def greeted(barrier):
    pl.semaphore_wait(barrier, NARROW + WIDE - 2)


def loop(count, fn):
    def body(i, carry):
        fn(i)
        return carry

    lax.fori_loop(0, count, body, 0)


class Names:
    def __init__(self, names, refs):
        for name, ref in zip(names, refs):
            setattr(self, name, ref)


class Round:
    def __init__(self, axis, size, me, src, dst, send, recv):
        self.axis, self.size, self.me = axis, size, me
        self.src, self.dst, self.send, self.recv = src, dst, send, recv

    def start(self, whole=False):
        def one(t):
            remote(
                self.src if whole else self.src.at[t],
                self.dst.at[self.me],
                self.send,
                self.recv,
                {self.axis: t},
            ).start()

        others(self.me, self.size, one)

    def all_of(self):
        part = self.dst.at[pl.ds(0, self.size - 1)]
        return remote(part, part, self.send, self.recv, {self.axis: lax.rem(self.me + 1, self.size)})

    def arrived(self):
        self.all_of().wait_recv()

    def sent(self):
        self.all_of().wait_send()


FORWARD = dict(
    ys=pltpu.VMEM((CHUNKS, NARROW, ROWS, 1024), F32),
    yr=pltpu.VMEM((CHUNKS, NARROW, ROWS, 1024), F32),
    xs=pltpu.VMEM((WIDE, 8, 128), F32),
    xr=pltpu.VMEM((WIDE, 8, 128), F32),
    ms=pltpu.VMEM((WIDE, 1, 128), F32),
    mr=pltpu.VMEM((WIDE, 1, 128), F32),
    ysem=pltpu.SemaphoreType.DMA((2, CHUNKS)),
    xsem=pltpu.SemaphoreType.DMA((2,)),
    msem=pltpu.SemaphoreType.DMA((2,)),
)

INVERSE = dict(
    ns=pltpu.VMEM((WIDE, 1, 128), F32),
    nr=pltpu.VMEM((WIDE, 1, 128), F32),
    vs=pltpu.VMEM((WIDE, 8, 128), F32),
    vr=pltpu.VMEM((WIDE, 8, 128), F32),
    as_=pltpu.VMEM((CHUNKS, ROWS, 1024), F32),
    ar=pltpu.VMEM((CHUNKS, NARROW, ROWS, 1024), F32),
    nsem=pltpu.SemaphoreType.DMA((2,)),
    vsem=pltpu.SemaphoreType.DMA((2,)),
    asem=pltpu.SemaphoreType.DMA((2, CHUNKS)),
)


def depth_forward(field, zf):
    full = dot(field.reshape(YL * C, NZ), zf)
    full = (full[:, :128] + full[:, 128:]).reshape(YL, 4, 8, 128)
    lane = lane_of((YL, 8, 128))
    low = jnp.where(lane < 32, full[:, 0], full[:, 1])
    high = jnp.where(lane < 96, full[:, 2], full[:, 3])
    return jnp.where(lane < 64, low, high)


class Forward:
    def __init__(self, s, own, n, w):
        self.s, self.own, self.n, self.w = s, own, n, w
        self.x = Round("wide", WIDE, w, own.xs, own.xr, own.xsem.at[0], own.xsem.at[1])
        self.m = Round("wide", WIDE, w, own.ms, own.mr, own.msem.at[0], own.msem.at[1])

    def y(self, q):
        o = self.own
        return Round("narrow", NARROW, self.n, o.ys.at[q], o.yr.at[q], o.ysem.at[0, q], o.ysem.at[1, q])

    def put_rows(self, i, depth):
        s = self.s
        s.d[...] = depth.reshape(YL * 8, 128)
        rows = pl.multiple_of(i * 64, 64)
        turned = pl.multiple_of(i * 64 + 32, 32)
        for c8 in range(8):
            part = s.d[pl.ds(c8, YL, stride=8), :]
            lanes = slice(c8 * 128, c8 * 128 + 128)
            s.rh[pl.ds(rows, 32), lanes], s.rl[pl.ds(rows, 32), lanes] = halves(part)
            s.rh[pl.ds(turned, 32), lanes], s.rl[pl.ds(turned, 32), lanes] = halves(turn(part))

    def send_chunk(self, q):
        s, o = self.s, self.own
        out = dot3(s.yf, s.rh[...], s.rl[...])
        o.ys[q] = out.reshape(NARROW, ROWS, 1024)
        o.yr[q, self.n] = o.ys[q, self.n]
        self.y(q).start()

    def sum_chunks(self):
        o = self.own
        for q in range(CHUNKS):
            self.y(q).arrived()
            total = o.yr[q, 0]
            for t in range(1, NARROW):
                total = total + o.yr[q, t]
            for k in range(KY):
                for c8 in range(8):
                    o.xs[k * 8 + c8, q * XC : q * XC + XC] = total[
                        k * XC : k * XC + XC, c8 * 128 : c8 * 128 + 128
                    ]
        o.xr[self.w] = o.xs[self.w]
        self.x.start()

    def to_owner(self, xf):
        o = self.own
        self.x.arrived()
        cells = o.xr[...].reshape(256, 128)
        hi, lo = halves(jnp.concatenate((cells, turn(cells)), axis=0))
        o.ms[...] = dot3(xf, hi, lo).reshape(WIDE, 1, 128)
        o.mr[self.w] = o.ms[self.w]
        self.m.start()

    def modes(self):
        self.m.arrived()
        return self.own.mr[...].reshape(WIDE, 128)

    def finish(self):
        loop(CHUNKS, lambda q: self.y(q).sent())
        self.x.sent()
        self.m.sent()


class Inverse:
    def __init__(self, s, own, n, w):
        self.s, self.own, self.n, self.w = s, own, n, w
        self.m = Round("wide", WIDE, w, own.ns, own.nr, own.nsem.at[0], own.nsem.at[1])
        self.x = Round("wide", WIDE, w, own.vs, own.vr, own.vsem.at[0], own.vsem.at[1])

    def y(self, q):
        o = self.own
        return Round("narrow", NARROW, self.n, o.as_.at[q], o.ar.at[q], o.asem.at[0, q], o.asem.at[1, q])

    def start(self, modes):
        o = self.own
        o.ns[...] = modes.reshape(WIDE, 1, 128)
        o.nr[self.w] = o.ns[self.w]
        self.m.start()

    def to_cells(self, xi):
        o = self.own
        self.m.arrived()
        modes = o.nr[...].reshape(WIDE, 128)
        hi, lo = halves(jnp.concatenate((modes, turn(modes)), axis=0))
        o.vs[...] = dot3(xi, hi, lo).reshape(WIDE, 8, 128)
        o.vr[self.w] = o.vs[self.w]
        self.x.start()

    def gather(self):
        o = self.own
        self.x.arrived()
        for q in range(CHUNKS):
            for k in range(KY):
                for c8 in range(8):
                    o.as_[q, k * XC : k * XC + XC, c8 * 128 : c8 * 128 + 128] = o.vr[
                        k * 8 + c8, q * XC : q * XC + XC
                    ]
            o.ar[q, self.n] = o.as_[q]
            self.y(q).start(whole=True)

    def chunk(self, q):
        s, o = self.s, self.own
        self.y(q).arrived()
        columns = []
        for c8 in range(8):
            part = o.ar[q, :, :, c8 * 128 : c8 * 128 + 128].reshape(NARROW * ROWS, 128)
            columns.append(jnp.concatenate((part, turn(part)), axis=0))
        hi, lo = halves(jnp.concatenate(columns, axis=1))
        out = dot3(s.yi, hi, lo)
        for i in range(XC):
            for c8 in range(8):
                s.s[pl.ds(i * 256 + c8, YL, stride=8), :] = out[
                    i * YL : i * YL + YL, c8 * 128 : c8 * 128 + 128
                ]

    def field_row(self, i, zi):
        s = self.s
        hi, lo = halves(s.s[pl.ds(pl.multiple_of(i * 256, 256), 256), :])
        both = jnp.concatenate((hi, lo, hi), axis=1)
        for g in range(4):
            s.field[:, g] = dot(both, zi[g]).reshape(YL, 8, NZ)

    def finish(self):
        self.m.sent()
        self.x.sent()
        loop(CHUNKS, lambda q: self.y(q).sent())


def fold_point(full):
    row = lax.broadcasted_iota(jnp.int32, full.shape, 0) // 32
    full = jnp.where(row == lane_of(full.shape) // 32, full, 0.0)
    total = full[0:32]
    for y in range(1, 8):
        total = total + full[y * 32 : y * 32 + 32]
    total = total[:, :128] + total[:, 128:]
    total = total + pltpu.roll(total, 64, 1)
    total = total + pltpu.roll(total, 32, 1)
    lane = lane_of((8, 128))
    low = jnp.where(lane < 32, total[0:8], total[8:16])
    high = jnp.where(lane < 96, total[16:24], total[24:32])
    return jnp.where(lane < 64, low, high)


def gelu_slope(u):
    k = math.sqrt(2.0 / math.pi)
    square = u * u
    h = 0.5 * jnp.tanh(u * (k + (k * 0.044715) * square)) + 0.5
    return h + h * (1.0 - h) * (u * (2.0 * k + (6.0 * k * 0.044715) * square))


def by_channel(rows):
    return jnp.concatenate(
        [
            pltpu.roll(rows[k * 8 : k * 8 + 8], (128 - 32 * g) % 128, 1)
            for k in range(KY)
            for g in range(4)
        ],
        axis=0,
    )


def by_group(pieces):
    lane = lane_of((8, 128))
    rows = []
    for k in range(KY):
        low = jnp.where(lane < 32, pieces(k, 0), pieces(k, 1))
        high = jnp.where(lane < 96, pieces(k, 2), pieces(k, 3))
        rows.append(jnp.where(lane < 64, low, high))
    return jnp.concatenate(rows, axis=0)


def mix_modes(s, modes):
    def body(kz, columns):
        for k in range(KY):
            rows = columns[k * C : k * C + C]
            real, imag = rows[:, 0:1], rows[:, M : M + 1]
            w_real, w_imag = s.weight[0, k, kz].astype(F32), s.weight[1, k, kz].astype(F32)
            s.mt[k, pl.ds(kz, 1), :C] = jnp.sum(real * w_real - imag * w_imag, axis=0, keepdims=True)
            s.mt[k, pl.ds(kz + M, 1), :C] = jnp.sum(
                real * w_imag + imag * w_real, axis=0, keepdims=True
            )
        return pltpu.roll(columns, 127, 1)

    s.mt[...] = jnp.zeros_like(s.mt)
    lax.fori_loop(0, M, body, by_channel(modes))
    turned = s.mt[...].reshape(KY * 2 * M, 128).T
    return by_group(
        lambda k, g: pltpu.roll(turned[g * 8 : g * 8 + 8], (128 + 32 * (g - k)) % 128, 1)
    )


def mix_back(s, grads):
    turned = by_channel(grads).T
    for k in range(KY):
        s.gt[k] = pltpu.roll(turned[: 2 * M], (128 - 32 * k) % 128, 1)
    lane = lane_of((C, 128))

    def body(kz, totals):
        out = []
        for k in range(KY):
            real, imag = s.gt[k, pl.ds(kz, 1), :C], s.gt[k, pl.ds(kz + M, 1), :C]
            w_real, w_imag = s.weight[0, k, kz].astype(F32), s.weight[1, k, kz].astype(F32)
            first = jnp.sum(real * w_real + imag * w_imag, axis=1, keepdims=True)
            second = jnp.sum(imag * w_real - real * w_imag, axis=1, keepdims=True)
            out.append(jnp.where(lane == kz, first, jnp.where(lane == kz + M, second, totals[k])))
        return tuple(out)

    totals = lax.fori_loop(0, M, body, tuple(jnp.zeros((C, 128), F32) for _ in range(KY)))
    return by_group(lambda k, g: pltpu.roll(totals[k][g * 8 : g * 8 + 8], 32 * g, 1))


def outer_modes(s, modes):
    def body(kz, columns):
        for k in range(KY):
            rows = columns[k * C : k * C + C]
            real, imag = rows[:, 0:1], rows[:, M : M + 1]
            g_real, g_imag = s.gt[k, pl.ds(kz, 1), :C], s.gt[k, pl.ds(kz + M, 1), :C]
            s.sg[0, k, kz] = real * g_real + imag * g_imag
            s.sg[1, k, kz] = real * g_imag - imag * g_real
        return pltpu.roll(columns, 127, 1)

    lax.fori_loop(0, M, body, by_channel(modes))


def kernel(
    names,
    act_hbm,
    cot_hbm,
    point_ref,
    bias_ref,
    weight_hbm,
    yf_hbm,
    yi_hbm,
    xf_ref,
    xi_ref,
    zf_ref,
    ziw_ref,
    zi1_ref,
    out_hbm,
    point_grad_ref,
    bias_grad_ref,
    sg_hbm,
    *refs,
):
    s = Names(names, refs)
    n, w = lax.axis_index("narrow"), lax.axis_index("wide")

    def group(prefix, keys):
        keys = tuple(keys)
        return Names(keys, [getattr(s, prefix + key) for key in keys])

    ahead = Forward(s, group("f1_", FORWARD), n, w)
    grad = Forward(s, group("f2_", FORWARD), n, w)
    mixed_in = Inverse(s, group("i1_", INVERSE), n, w)
    back_in = Inverse(s, group("i2_", INVERSE), n, w)

    def act_copy(x):
        return pltpu.make_async_copy(act_hbm.at[x], s.act.at[x], s.act_sem.at[x])

    def cot_copy(x):
        return pltpu.make_async_copy(cot_hbm.at[x], s.cot.at[x], s.cot_sem.at[x])

    def out_copy(x):
        return pltpu.make_async_copy(s.out.at[x], out_hbm.at[x], s.out_sem.at[x])

    table_in = [
        pltpu.make_async_copy(yf_hbm.at[n], s.yf, s.table_sem.at[0]),
        pltpu.make_async_copy(yi_hbm.at[n], s.yi, s.table_sem.at[1]),
    ]
    weight_copy = pltpu.make_async_copy(weight_hbm.at[:, 0], s.weight, s.table_sem.at[2])
    sg_copy = pltpu.make_async_copy(s.sg, sg_hbm.at[:, 0], s.table_sem.at[3])
    barrier = greet(n, w)
    loop(XL, lambda x: act_copy(x).start())
    for copy in table_in:
        copy.start()
    weight_copy.start()
    loop(XL, lambda x: cot_copy(x).start())
    for copy in table_in:
        copy.wait()

    def forward_chunk(q):
        def row(i):
            x = q * XC + i
            act_copy(x).wait()
            ahead.put_rows(i, depth_forward(s.act[x], zf_ref[...]))

        loop(XC, row)

        @pl.when(q == 0)
        def _():
            greeted(barrier)

        ahead.send_chunk(q)

    loop(CHUNKS, forward_chunk)

    row = lax.broadcasted_iota(jnp.int32, (256, 32), 0)
    pick = lax.rem(row, 32) == lane_of((256, 32))
    ones = jnp.where(pick, 1.0, 0.0).astype(BF16)
    bias_rows = jnp.sum(jnp.where(pick, bias_ref[...], 0.0), axis=1, keepdims=True)
    same = lax.broadcasted_iota(jnp.int32, (256, 256), 0) // 32 == lane_of((256, 256)) // 32
    tall = dot(ones, point_ref[...]).astype(BF16)
    s.mix_back[...] = jnp.where(same, dot_t(tall, ones), 0.0).astype(BF16)
    tall = dot_t(ones, point_ref[...]).astype(BF16)
    s.mix[...] = jnp.where(same, dot_t(tall, ones), 0.0).astype(BF16)

    def blocks(fn):
        def one(i):
            fn(i // 4, pl.ds(pl.multiple_of(lax.rem(i, 4) * 8, 8), 8))

        loop(4 * XL, one)

    def mix_block(x, ys):
        point = dot(s.mix[...], s.act[x, ys].reshape(256, NZ)) + bias_rows
        s.point[x, ys] = point.reshape(8, C, NZ)

    blocks(mix_block)
    ahead.sum_chunks()
    ahead.to_owner(xf_ref)
    weight_copy.wait()
    mixed_in.start(mix_modes(s, ahead.modes()))
    s.bs[...] = jnp.zeros_like(s.bs)
    s.pg[...] = jnp.zeros_like(s.pg)
    mixed_in.to_cells(xi_ref)
    mixed_in.gather()

    def middle_chunk(q):
        mixed_in.chunk(q)

        def row(i):
            x = q * XC + i
            cot_copy(x).wait()
            mixed_in.field_row(i, ziw_ref)

            def block(b):
                ys = pl.ds(pl.multiple_of(b * 8, 8), 8)
                preact = s.field[ys].reshape(256, NZ) + s.point[x, ys].reshape(256, NZ)
                cot = s.cot[x, ys].reshape(256, NZ).astype(F32)
                pre = (cot * gelu_slope(preact)).astype(BF16)
                s.pre[x, ys] = pre.reshape(8, C, NZ)

            loop(4, block)
            depth = depth_forward(s.pre[x], zf_ref[...])
            s.bs[...] += jnp.sum(depth, axis=0)
            grad.put_rows(i, depth)

        loop(XC, row)
        grad.send_chunk(q)

    loop(CHUNKS, middle_chunk)

    def back_block(x, ys):
        pre = s.pre[x, ys].reshape(256, NZ)
        s.pg[...] += dot_t(s.act[x, ys].reshape(256, NZ), pre)
        s.point[x, ys] = dot(s.mix_back[...], pre).reshape(8, C, NZ)

    blocks(back_block)
    s.ps[0:8] = fold_point(s.pg[...])
    s.ps[8:16] = s.bs[...]
    s.pr[n] = s.ps[...]
    grad.sum_chunks()
    narrow_sum = Round("narrow", NARROW, n, s.ps, s.pr, s.psem.at[0], s.psem.at[1])
    narrow_sum.start(whole=True)
    grad.to_owner(xf_ref)
    narrow_sum.arrived()
    total = s.pr[0]
    for t in range(1, NARROW):
        total = total + s.pr[t]
    s.ts[...] = total
    s.tr[w] = total
    rows = grad.modes()
    depth_weight = jnp.where(lax.rem(lane_of(rows.shape), 16) == 0, 1.0, 2.0)
    grads = rows * depth_weight
    back_in.start(mix_back(s, grads))
    outer_modes(s, ahead.own.mr[...].reshape(WIDE, 128))
    sg_copy.start()
    back_in.to_cells(xi_ref)
    wide_sum = Round("wide", WIDE, w, s.ts, s.tr, s.tsem.at[0], s.tsem.at[1])
    back_in.gather()
    wide_sum.start(whole=True)

    def last_chunk(q):
        back_in.chunk(q)

        def row(i):
            x = q * XC + i
            back_in.field_row(i, zi1_ref)

            def block(b):
                ys = pl.ds(pl.multiple_of(b * 8, 8), 8)
                out = s.field[ys].reshape(256, NZ) + s.point[x, ys].reshape(256, NZ)
                s.out[x, ys] = out.astype(BF16).reshape(8, C, NZ)

            loop(4, block)
            out_copy(x).start()

        loop(XC, row)

    loop(CHUNKS, last_chunk)
    wide_sum.arrived()
    total = s.tr[0]
    for t in range(1, WIDE):
        total = total + s.tr[t]
    for g in range(4):
        point_grad_ref[g * 8 : g * 8 + 8] = SCALE * total[0:8, g * 32 : g * 32 + C]
    row, lane = lax.broadcasted_iota(jnp.int32, (8, C), 0), lane_of((8, C))
    bias_grad = jnp.zeros((8, C), F32)
    for g in range(4):
        bias_grad = jnp.where(lane == g * 8 + row, total[8:16, g * 32 : g * 32 + 1], bias_grad)
    bias_grad_ref[...] = SCALE * jnp.sum(bias_grad, axis=0, keepdims=True)
    for part in (ahead, grad, mixed_in, back_in):
        part.finish()
    narrow_sum.sent()
    wide_sum.sent()
    sg_copy.wait()
    loop(XL, lambda x: out_copy(x).wait())


VM = pl.BlockSpec(memory_space=pltpu.VMEM)
HB = pl.BlockSpec(memory_space=pl.ANY)
FIELD = (XL, YL, C, NZ)


def local(activations, cotangent, point_weight, bias, spectral_weight):
    tabs = {name: jnp.asarray(value) for name, value in tables().items()}
    scratch = dict(
        act=pltpu.VMEM(FIELD, BF16),
        cot=pltpu.VMEM(FIELD, BF16),
        pre=pltpu.VMEM(FIELD, BF16),
        out=pltpu.VMEM(FIELD, BF16),
        point=pltpu.VMEM(FIELD, F32),
        field=pltpu.VMEM((YL, 4, 8, NZ), F32),
        d=pltpu.VMEM((256, 128), F32),
        rh=pltpu.VMEM((64 * XC, 1024), BF16),
        rl=pltpu.VMEM((64 * XC, 1024), BF16),
        s=pltpu.VMEM((XC * 256, 128), F32),
        yf=pltpu.VMEM((2, 32 * XC, 64 * XC), BF16),
        yi=pltpu.VMEM((2, 32 * XC, 64 * XC), BF16),
        mix=pltpu.VMEM((256, 256), BF16),
        mix_back=pltpu.VMEM((256, 256), BF16),
        weight=pltpu.VMEM((2, KY, M, C, C), BF16),
        sg=pltpu.VMEM((2, KY, M, C, C), F32),
        mt=pltpu.VMEM((KY, 2 * M, 128), F32),
        gt=pltpu.VMEM((KY, 2 * M, 128), F32),
        pg=pltpu.VMEM((256, 256), F32),
        bs=pltpu.VMEM((8, 128), F32),
        ps=pltpu.VMEM((16, 128), F32),
        pr=pltpu.VMEM((NARROW, 16, 128), F32),
        ts=pltpu.VMEM((16, 128), F32),
        tr=pltpu.VMEM((WIDE, 16, 128), F32),
        act_sem=pltpu.SemaphoreType.DMA((XL,)),
        cot_sem=pltpu.SemaphoreType.DMA((XL,)),
        out_sem=pltpu.SemaphoreType.DMA((XL,)),
        table_sem=pltpu.SemaphoreType.DMA((4,)),
        psem=pltpu.SemaphoreType.DMA((2,)),
        tsem=pltpu.SemaphoreType.DMA((2,)),
    )
    for prefix, group in (("f1_", FORWARD), ("f2_", FORWARD), ("i1_", INVERSE), ("i2_", INVERSE)):
        scratch.update({prefix + key: value for key, value in group.items()})
    input_grad, point_grad, bias_grad, spectral_grad = pl.pallas_call(
        functools.partial(kernel, tuple(scratch)),
        name="layer_backward",
        in_specs=[HB, HB, VM, VM, HB, HB, HB, VM, VM, VM, VM, VM],
        out_specs=[HB, VM, VM, HB],
        out_shape=[
            jax.ShapeDtypeStruct(FIELD, BF16),
            jax.ShapeDtypeStruct((C, C), F32),
            jax.ShapeDtypeStruct((1, C), F32),
            jax.ShapeDtypeStruct((2, 1, KY, M, C, C), F32),
        ],
        scratch_shapes=tuple(scratch.values()),
        compiler_params=pltpu.CompilerParams(
            collective_id=0, has_side_effects=True, vmem_limit_bytes=56 * 1024 * 1024
        ),
    )(
        activations,
        cotangent,
        point_weight,
        bias[None],
        spectral_weight,
        *(tabs[name] for name in ("yf", "yi", "xf", "xi", "zf", "ziw", "zi1")),
    )

    return (input_grad, point_grad, bias_grad.reshape(C), spectral_grad)


def solution(mesh):
    return jax.shard_map(
        local,
        mesh=mesh,
        in_specs=(
            P("wide", "narrow", None, None),
            P("wide", "narrow", None, None),
            P(),
            P(),
            P(None, "wide", "narrow", None, None, None),
        ),
        out_specs=(
            P("wide", "narrow", None, None),
            P(),
            P(),
            P(None, "wide", "narrow", None, None, None),
        ),
        check_vma=False,
    )
```

```python
import functools
import math

import jax
import jax.numpy as jnp
import ml_dtypes
import numpy as np
from jax import lax
from jax.experimental import pallas as pl
from jax.experimental.pallas import tpu as pltpu
from jax.sharding import PartitionSpec as P

WIDE = 32
NARROW = 8
M = 16
C = 32
NZ = 256
XL = 8
YL = 32
KY = 4
XC = 2
CHUNKS = XL // XC
ROWS = KY * XC
SCALE = 1.0 / 4096.0

F32 = jnp.float32
BF16 = jnp.bfloat16


def kept(j):
    return np.where(j < 16, j, 224 + j)


def trig(freqs, cells):
    angle = (np.outer(freqs, cells) % 256) * (2.0 * math.pi / 256.0)
    return np.cos(angle), np.sin(angle)


def split_np(table):
    hi = table.astype(np.float32).astype(ml_dtypes.bfloat16)
    lo = (table - hi.astype(np.float64)).astype(np.float32).astype(ml_dtypes.bfloat16)
    return hi, lo


@functools.lru_cache(maxsize=None)
def tables():
    freqs = kept(np.arange(32))
    cos_a, sin_a = trig(freqs, np.arange(256))
    cos_z, sin_z = trig(np.arange(M), np.arange(NZ))
    eye_x = np.eye(XC)
    cy = cos_a.reshape(NARROW, KY, NARROW, YL)
    sy = sin_a.reshape(NARROW, KY, NARROW, YL)
    both = np.stack((cy, sy))
    yf = np.einsum("dtkny,xu->ntkxudy", both, eye_x).reshape(NARROW, 32 * XC, 64 * XC)
    both = np.stack((cy, -sy))
    yi = np.einsum("dtkny,xu->nxydtku", both, eye_x).reshape(NARROW, 32 * XC, 64 * XC)
    xf = np.concatenate((cos_a, sin_a), axis=1) * SCALE
    xi = np.concatenate((cos_a.T, -sin_a.T), axis=1)
    parts = np.stack((cos_z, -sin_z)).reshape(2, 8, 2, NZ)
    zf = np.broadcast_to(parts.transpose(3, 1, 0, 2)[:, :, None], (NZ, 8, 4, 2, 2)).reshape(NZ, 128)
    depth = np.where(np.arange(M) == 0, 1.0, 2.0)[:, None]

    def inverse_z(weights):
        one = (parts * weights.reshape(1, 8, 2, 1)).transpose(1, 0, 2, 3) * SCALE
        full = np.zeros((4, 8, 4, 2, 2, NZ))
        for g in range(4):
            full[g, :, g] = one
        hi, lo = split_np(full.reshape(4, 128, NZ))
        return np.concatenate((hi, hi, lo), axis=1)

    eye = np.eye
    pick_c = np.einsum(
        "gG,pP,kK,co->cgpkPKGo", eye(4), eye(2), eye(2), np.ones((8, C))
    ).reshape(128, 512)
    pick_o = np.einsum(
        "hgo,pP,kK,G->hgpkPKGo", eye(C).reshape(4, 8, C).transpose(1, 0, 2), eye(2), eye(2), np.ones(4)
    ).reshape(128, 512)
    return dict(
        yf=np.stack(split_np(yf), axis=1),
        yi=np.stack(split_np(yi), axis=1),
        xf=np.stack(split_np(xf)),
        xi=np.stack(split_np(xi)),
        zf=np.concatenate(split_np(zf), axis=1),
        ziw=inverse_z(depth),
        zi1=inverse_z(np.ones((M, 1))),
        pick_c=pick_c.astype(ml_dtypes.bfloat16),
        pick_o=pick_o.astype(ml_dtypes.bfloat16),
    )


def dot(a, b):
    return jnp.dot(a, b, preferred_element_type=F32)


def dot_t(a, b):
    return lax.dot_general(a, b, (((1,), (1,)), ((), ())), preferred_element_type=F32)


def halves(x):
    hi = x.astype(BF16)
    return hi, (x - hi.astype(F32)).astype(BF16)


def dot3(table, hi, lo):
    t_hi, t_lo = table[0], table[1]
    return dot(t_hi, hi) + (dot(t_hi, lo) + dot(t_lo, hi))


def lane_of(shape):
    return lax.broadcasted_iota(jnp.int32, shape, len(shape) - 1)


def turn(x):
    real = lax.rem(lane_of(x.shape), 4) < 2
    return jnp.where(real, pltpu.roll(x, 126, x.ndim - 1), -pltpu.roll(x, 2, x.ndim - 1))


def exchange(tiles):
    tiles = list(tiles)
    group = lane_of(tiles[0].shape) // 16
    for step in (1, 2, 4):
        high = lax.rem(group // step, 2) == 1
        for t in range(8):
            if t & step == 0:
                one, two = tiles[t], tiles[t + step]
                tiles[t] = jnp.where(high, pltpu.roll(two, 16 * step, 1), one)
                tiles[t + step] = jnp.where(high, two, pltpu.roll(one, 128 - 16 * step, 1))
    return tiles


def remote(src, dst, send, recv, device):
    return pltpu.make_async_remote_copy(
        src_ref=src,
        dst_ref=dst,
        send_sem=send,
        recv_sem=recv,
        device_id=device,
        device_id_type=pl.DeviceIdType.MESH,
    )


def others(me, size, fn):
    def body(k, carry):
        fn(lax.rem(me + k, size))
        return carry

    lax.fori_loop(1, size, body, 0)


def greet(n, w):
    barrier = pltpu.get_barrier_semaphore()

    def signal(axis):
        return lambda t: pl.semaphore_signal(
            barrier, inc=1, device_id={axis: t}, device_id_type=pl.DeviceIdType.MESH
        )

    others(n, NARROW, signal("narrow"))
    others(w, WIDE, signal("wide"))
    return barrier


def greeted(barrier):
    pl.semaphore_wait(barrier, NARROW + WIDE - 2)


def loop(count, fn):
    def body(i, carry):
        fn(i)
        return carry

    lax.fori_loop(0, count, body, 0)


class Names:
    def __init__(self, names, refs):
        for name, ref in zip(names, refs):
            setattr(self, name, ref)


class Round:
    def __init__(self, axis, size, me, src, dst, send, recv):
        self.axis, self.size, self.me = axis, size, me
        self.src, self.dst, self.send, self.recv = src, dst, send, recv

    def start(self, whole=False):
        def one(t):
            remote(
                self.src if whole else self.src.at[t],
                self.dst.at[self.me],
                self.send,
                self.recv,
                {self.axis: t},
            ).start()

        others(self.me, self.size, one)

    def all_of(self):
        part = self.dst.at[pl.ds(0, self.size - 1)]
        return remote(part, part, self.send, self.recv, {self.axis: lax.rem(self.me + 1, self.size)})

    def arrived(self):
        self.all_of().wait_recv()

    def sent(self):
        self.all_of().wait_send()


FORWARD = dict(
    ys=pltpu.VMEM((CHUNKS, NARROW, ROWS, 1024), F32),
    yr=pltpu.VMEM((CHUNKS, NARROW, ROWS, 1024), F32),
    xs=pltpu.VMEM((WIDE, 8, 128), F32),
    xr=pltpu.VMEM((WIDE, 8, 128), F32),
    ms=pltpu.VMEM((WIDE, 1, 128), F32),
    mr=pltpu.VMEM((WIDE, 1, 128), F32),
    ysem=pltpu.SemaphoreType.DMA((2, CHUNKS)),
    xsem=pltpu.SemaphoreType.DMA((2,)),
    msem=pltpu.SemaphoreType.DMA((2,)),
)

INVERSE = dict(
    vs=pltpu.VMEM((WIDE, 8, 128), F32),
    vr=pltpu.VMEM((WIDE, 8, 128), F32),
    as_=pltpu.VMEM((CHUNKS, ROWS, 1024), F32),
    ar=pltpu.VMEM((CHUNKS, NARROW, ROWS, 1024), F32),
    vsem=pltpu.SemaphoreType.DMA((2,)),
    asem=pltpu.SemaphoreType.DMA((2, CHUNKS)),
)


def depth_forward(field, zf):
    full = dot(field.reshape(YL * C, NZ), zf)
    full = (full[:, :128] + full[:, 128:]).reshape(YL, 4, 8, 128)
    group = lax.rem(lane_of((YL, 8, 128)) // 4, 4)
    low = jnp.where(group == 0, full[:, 0], full[:, 1])
    high = jnp.where(group == 2, full[:, 2], full[:, 3])
    return jnp.where(group < 2, low, high)


class Forward:
    def __init__(self, s, own, n, w):
        self.s, self.own, self.n, self.w = s, own, n, w
        self.x = Round("wide", WIDE, w, own.xs, own.xr, own.xsem.at[0], own.xsem.at[1])
        self.m = Round("wide", WIDE, w, own.ms, own.mr, own.msem.at[0], own.msem.at[1])

    def y(self, q):
        o = self.own
        return Round("narrow", NARROW, self.n, o.ys.at[q], o.yr.at[q], o.ysem.at[0, q], o.ysem.at[1, q])

    def put_rows(self, i, depth):
        s = self.s
        s.d[...] = depth.reshape(YL * 8, 128)
        rows = pl.multiple_of(i * 64, 64)
        turned = pl.multiple_of(i * 64 + 32, 32)
        for c8 in range(8):
            part = s.d[pl.ds(c8, YL, stride=8), :]
            lanes = slice(c8 * 128, c8 * 128 + 128)
            s.rh[pl.ds(rows, 32), lanes], s.rl[pl.ds(rows, 32), lanes] = halves(part)
            s.rh[pl.ds(turned, 32), lanes], s.rl[pl.ds(turned, 32), lanes] = halves(turn(part))

    def send_chunk(self, q):
        s, o = self.s, self.own
        out = dot3(s.yf, s.rh[...], s.rl[...])
        o.ys[q] = out.reshape(NARROW, ROWS, 1024)
        o.yr[q, self.n] = o.ys[q, self.n]
        self.y(q).start()

    def sum_chunks(self):
        o = self.own
        for q in range(CHUNKS):
            self.y(q).arrived()
            total = o.yr[q, 0]
            for t in range(1, NARROW):
                total = total + o.yr[q, t]
            tiles = exchange([total[:, t * 128 : t * 128 + 128] for t in range(8)])
            for k in range(KY):
                for t in range(8):
                    o.xs[k * 8 + t, q * XC : q * XC + XC] = tiles[t][k * XC : k * XC + XC]
        o.xr[self.w] = o.xs[self.w]
        self.x.start()

    def modes(self, xf):
        o = self.own
        self.x.arrived()
        cells = o.xr[...].reshape(256, 128)
        hi, lo = halves(jnp.concatenate((cells, turn(cells)), axis=0))
        return dot3(xf, hi, lo)

    def to_owner(self, modes):
        o = self.own
        o.ms[...] = modes.reshape(WIDE, 1, 128)
        o.mr[self.w] = o.ms[self.w]
        self.m.start()

    def owned(self):
        self.m.arrived()
        return self.own.mr[...].reshape(WIDE, 128)

    def finish(self):
        loop(CHUNKS, lambda q: self.y(q).sent())
        self.x.sent()
        self.m.sent()


class Inverse:
    def __init__(self, s, own, n, w):
        self.s, self.own, self.n, self.w = s, own, n, w
        self.x = Round("wide", WIDE, w, own.vs, own.vr, own.vsem.at[0], own.vsem.at[1])

    def y(self, q):
        o = self.own
        return Round("narrow", NARROW, self.n, o.as_.at[q], o.ar.at[q], o.asem.at[0, q], o.asem.at[1, q])

    def to_cells(self, modes, xi):
        o = self.own
        hi, lo = halves(jnp.concatenate((modes, turn(modes)), axis=0))
        o.vs[...] = dot3(xi, hi, lo).reshape(WIDE, 8, 128)
        o.vr[self.w] = o.vs[self.w]
        self.x.start()

    def gather(self):
        o = self.own
        self.x.arrived()
        tiles = [exchange([o.vr[k * 8 + t] for t in range(8)]) for k in range(KY)]
        for q in range(CHUNKS):
            for k in range(KY):
                for c8 in range(8):
                    o.as_[q, k * XC : k * XC + XC, c8 * 128 : c8 * 128 + 128] = tiles[k][c8][
                        q * XC : q * XC + XC
                    ]
            o.ar[q, self.n] = o.as_[q]
            self.y(q).start(whole=True)

    def chunk(self, q):
        s, o = self.s, self.own
        self.y(q).arrived()
        columns = []
        for c8 in range(8):
            part = o.ar[q, :, :, c8 * 128 : c8 * 128 + 128].reshape(NARROW * ROWS, 128)
            columns.append(jnp.concatenate((part, turn(part)), axis=0))
        hi, lo = halves(jnp.concatenate(columns, axis=1))
        out = dot3(s.yi, hi, lo)
        for i in range(XC):
            for c8 in range(8):
                s.s[pl.ds(i * 256 + c8, YL, stride=8), :] = out[
                    i * YL : i * YL + YL, c8 * 128 : c8 * 128 + 128
                ]

    def field_row(self, i, zi):
        s = self.s
        hi, lo = halves(s.s[pl.ds(pl.multiple_of(i * 256, 256), 256), :])
        both = jnp.concatenate((hi, lo, hi), axis=1)
        for g in range(4):
            s.field[:, g] = dot(both, zi[g]).reshape(YL, 8, NZ)

    def finish(self):
        self.x.sent()
        loop(CHUNKS, lambda q: self.y(q).sent())


def fold_point(full):
    row = lax.broadcasted_iota(jnp.int32, full.shape, 0) // 32
    full = jnp.where(row == lane_of(full.shape) // 32, full, 0.0)
    total = full[0:32]
    for y in range(1, 8):
        total = total + full[y * 32 : y * 32 + 32]
    total = total[:, :128] + total[:, 128:]
    total = total + pltpu.roll(total, 64, 1)
    total = total + pltpu.roll(total, 32, 1)
    lane = lane_of((8, 128))
    low = jnp.where(lane < 32, total[0:8], total[8:16])
    high = jnp.where(lane < 96, total[16:24], total[24:32])
    return jnp.where(lane < 64, low, high)


def gelu_slope(u):
    k = math.sqrt(2.0 / math.pi)
    square = u * u
    h = 0.5 * jnp.tanh(u * (k + (k * 0.044715) * square)) + 0.5
    return h + h * (1.0 - h) * (u * (2.0 * k + (6.0 * k * 0.044715) * square))


def select(rows, pick):
    hi, lo = halves(rows)
    return dot(hi, pick) + dot(lo, pick)


def gather_back(columns, pick):
    hi, lo = halves(columns)
    return dot_t(hi, pick) + dot_t(lo, pick)


def part_of(columns, part, k2):
    at = (2 * part + k2) * 128
    return columns[:, at : at + 128]


def own_channel(rows):
    row = lax.rem(lax.broadcasted_iota(jnp.int32, rows.shape, 0), 8)
    return jnp.where(lane_of(rows.shape) // 16 == row, rows, 0.0)


def over_rows(rows):
    lanes = rows.shape[1]
    return jnp.broadcast_to(rows[:, None], (WIDE, 8, lanes)).reshape(WIDE * 8, lanes)


def by_input(modes, pick_c):
    return select(own_channel(over_rows(modes)), pick_c)


def weight_of(wr):
    def at(part, k2):
        return wr[:, 2 * part + k2].reshape(WIDE * 8, 128)

    return at


def mix_modes(modes, weight, pick_c, pick_o):
    columns = by_input(modes, pick_c)
    real, imag = [], []
    for k2 in range(2):
        c_real, c_imag = part_of(columns, 0, k2), part_of(columns, 1, k2)
        w_real, w_imag = weight(0, k2), weight(1, k2)
        real.append(c_real * w_real - c_imag * w_imag)
        imag.append(c_real * w_imag + c_imag * w_real)
    full = jnp.concatenate(real + imag, axis=1).reshape(WIDE, 8, 512)
    return gather_back(jnp.sum(full, axis=1), pick_o)


def mix_back(grads, weight, pick_c, pick_o):
    columns = over_rows(select(grads, pick_o))
    real, imag = [], []
    for k2 in range(2):
        g_real, g_imag = part_of(columns, 0, k2), part_of(columns, 1, k2)
        w_real, w_imag = weight(0, k2), weight(1, k2)
        real.append(g_real * w_real + g_imag * w_imag)
        imag.append(g_imag * w_real - g_real * w_imag)
    full = own_channel(gather_back(jnp.concatenate(real + imag, axis=1), pick_c))
    return jnp.sum(full.reshape(WIDE, 8, 128), axis=1)


def outer_modes(s, modes, grads, pick_c, pick_o):
    first = by_input(modes, pick_c)
    second = over_rows(select(grads, pick_o))
    for k2 in range(2):
        c_real, c_imag = part_of(first, 0, k2), part_of(first, 1, k2)
        g_real, g_imag = part_of(second, 0, k2), part_of(second, 1, k2)
        for part, value in enumerate(
            (c_real * g_real + c_imag * g_imag, c_real * g_imag - c_imag * g_real)
        ):
            for g in range(4):
                moved = pltpu.roll(value, (128 - 32 * g) % 128, 1) if g else value
                s.sg[part, :, :, k2, g * 8 : g * 8 + 8, :] = moved[:, :C].reshape(KY, 8, 8, C)


def pack_weight(s, n, w):
    def one(k):
        for part in range(2):
            for k2 in range(2):
                full = s.weight[part, k, :, k2].astype(F32)
                tile = jnp.concatenate([full[:, g * 8 : g * 8 + 8] for g in range(4)], axis=-1)
                s.ws[pl.ds(pl.multiple_of(k * 8, 8), 8), 2 * part + k2] = tile

    loop(KY, one)
    s.wr[w] = s.ws[w]


def kernel(
    names,
    act_hbm,
    cot_hbm,
    point_ref,
    bias_ref,
    weight_hbm,
    yf_hbm,
    yi_hbm,
    xf_ref,
    xi_ref,
    zf_ref,
    ziw_ref,
    zi1_ref,
    pick_c_ref,
    pick_o_ref,
    out_hbm,
    point_grad_ref,
    bias_grad_ref,
    sg_hbm,
    *refs,
):
    s = Names(names, refs)
    n, w = lax.axis_index("narrow"), lax.axis_index("wide")

    def group(prefix, keys):
        keys = tuple(keys)
        return Names(keys, [getattr(s, prefix + key) for key in keys])

    ahead = Forward(s, group("f1_", FORWARD), n, w)
    grad = Forward(s, group("f2_", FORWARD), n, w)
    mixed_in = Inverse(s, group("i1_", INVERSE), n, w)
    back_in = Inverse(s, group("i2_", INVERSE), n, w)

    def act_copy(x):
        return pltpu.make_async_copy(act_hbm.at[x], s.act.at[x], s.act_sem.at[x])

    def cot_copy(x):
        return pltpu.make_async_copy(cot_hbm.at[x], s.cot.at[x], s.cot_sem.at[x])

    def out_copy(x):
        return pltpu.make_async_copy(s.out.at[x], out_hbm.at[x], s.out_sem.at[x])

    table_in = [
        pltpu.make_async_copy(yf_hbm.at[n], s.yf, s.table_sem.at[0]),
        pltpu.make_async_copy(yi_hbm.at[n], s.yi, s.table_sem.at[1]),
    ]
    weight_copy = pltpu.make_async_copy(weight_hbm.at[:, 0], s.weight, s.table_sem.at[2])
    sg_copy = pltpu.make_async_copy(s.sg, sg_hbm.at[:, 0], s.table_sem.at[3])
    barrier = greet(n, w)
    loop(XL, lambda x: act_copy(x).start())
    for copy in table_in:
        copy.start()
    weight_copy.start()
    loop(XL, lambda x: cot_copy(x).start())
    for copy in table_in:
        copy.wait()

    def forward_chunk(q):
        def row(i):
            x = q * XC + i
            act_copy(x).wait()
            ahead.put_rows(i, depth_forward(s.act[x], zf_ref[...]))

        loop(XC, row)

        @pl.when(q == 0)
        def _():
            greeted(barrier)

        ahead.send_chunk(q)

    loop(CHUNKS, forward_chunk)

    row = lax.broadcasted_iota(jnp.int32, (256, 32), 0)
    pick = lax.rem(row, 32) == lane_of((256, 32))
    ones = jnp.where(pick, 1.0, 0.0).astype(BF16)
    bias_rows = jnp.sum(jnp.where(pick, bias_ref[...], 0.0), axis=1, keepdims=True)
    same = lax.broadcasted_iota(jnp.int32, (256, 256), 0) // 32 == lane_of((256, 256)) // 32
    tall = dot(ones, point_ref[...]).astype(BF16)
    s.mix_back[...] = jnp.where(same, dot_t(tall, ones), 0.0).astype(BF16)
    tall = dot_t(ones, point_ref[...]).astype(BF16)
    s.mix[...] = jnp.where(same, dot_t(tall, ones), 0.0).astype(BF16)

    def blocks(fn, low, high):
        def one(i, carry):
            fn(i // 4, pl.ds(pl.multiple_of(lax.rem(i, 4) * 8, 8), 8))
            return carry

        lax.fori_loop(low, high, one, 0)

    def mix_block(x, ys):
        point = dot(s.mix[...], s.act[x, ys].reshape(256, NZ)) + bias_rows
        s.point[x, ys] = point.reshape(8, C, NZ)

    weight_copy.wait()
    pack_weight(s, n, w)
    weight_round = Round("wide", WIDE, w, s.ws, s.wr, s.wsem.at[0], s.wsem.at[1])
    weight_round.start()
    pick_c, pick_o = pick_c_ref[...], pick_o_ref[...]
    weight = weight_of(s.wr)
    blocks(mix_block, 0, 20)
    ahead.sum_chunks()
    blocks(mix_block, 20, 26)
    weight_round.arrived()
    coeffs = ahead.modes(xf_ref)
    mixed_in.to_cells(mix_modes(coeffs, weight, pick_c, pick_o), xi_ref)
    ahead.to_owner(coeffs)
    s.bs[...] = jnp.zeros_like(s.bs)
    s.pg[...] = jnp.zeros_like(s.pg)
    blocks(mix_block, 26, 4 * XL)
    mixed_in.gather()

    def middle_chunk(q):
        mixed_in.chunk(q)

        def row(i):
            x = q * XC + i
            cot_copy(x).wait()
            mixed_in.field_row(i, ziw_ref)

            def block(b):
                ys = pl.ds(pl.multiple_of(b * 8, 8), 8)
                preact = s.field[ys].reshape(256, NZ) + s.point[x, ys].reshape(256, NZ)
                cot = s.cot[x, ys].reshape(256, NZ).astype(F32)
                pre = (cot * gelu_slope(preact)).astype(BF16)
                s.pre[x, ys] = pre.reshape(8, C, NZ)

            loop(4, block)
            depth = depth_forward(s.pre[x], zf_ref[...])
            s.bs[...] += jnp.sum(depth, axis=0)
            grad.put_rows(i, depth)

        loop(XC, row)
        grad.send_chunk(q)

    loop(CHUNKS, middle_chunk)

    def back_block(x, ys):
        pre = s.pre[x, ys].reshape(256, NZ)
        s.pg[...] += dot_t(s.act[x, ys].reshape(256, NZ), pre)
        s.point[x, ys] = dot(s.mix_back[...], pre).reshape(8, C, NZ)

    blocks(back_block, 0, 8)
    grad.sum_chunks()
    blocks(back_block, 8, 20)
    rows = grad.modes(xf_ref)
    first = lax.rem(w, 8) == 0
    grads = rows * jnp.where((lax.rem(lane_of(rows.shape), 2) == 0) & first, 1.0, 2.0)
    back_in.to_cells(mix_back(grads, weight, pick_c, pick_o), xi_ref)
    grad.to_owner(grads)
    blocks(back_block, 20, 4 * XL)
    s.ps[0:8] = fold_point(s.pg[...])
    s.ps[8:16] = s.bs[...]
    s.pr[n] = s.ps[...]
    back_in.gather()
    narrow_sum = Round("narrow", NARROW, n, s.ps, s.pr, s.psem.at[0], s.psem.at[1])
    narrow_sum.start(whole=True)
    outer_modes(s, ahead.owned(), grad.owned(), pick_c, pick_o)
    sg_copy.start()
    narrow_sum.arrived()
    total = s.pr[0]
    for t in range(1, NARROW):
        total = total + s.pr[t]
    s.ts[...] = total
    s.tr[w] = total
    wide_sum = Round("wide", WIDE, w, s.ts, s.tr, s.tsem.at[0], s.tsem.at[1])
    wide_sum.start(whole=True)

    def last_chunk(q):
        back_in.chunk(q)

        def row(i):
            x = q * XC + i
            back_in.field_row(i, zi1_ref)

            def block(b):
                ys = pl.ds(pl.multiple_of(b * 8, 8), 8)
                out = s.field[ys].reshape(256, NZ) + s.point[x, ys].reshape(256, NZ)
                s.out[x, ys] = out.astype(BF16).reshape(8, C, NZ)

            loop(4, block)
            out_copy(x).start()

        loop(XC, row)

    loop(CHUNKS, last_chunk)
    wide_sum.arrived()
    total = s.tr[0]
    for t in range(1, WIDE):
        total = total + s.tr[t]
    for g in range(4):
        point_grad_ref[g * 8 : g * 8 + 8] = SCALE * total[0:8, g * 32 : g * 32 + C]
    row, lane = lax.broadcasted_iota(jnp.int32, (8, C), 0), lane_of((8, C))
    bias_grad = jnp.zeros((8, C), F32)
    for g in range(4):
        bias_grad = jnp.where(lane == g * 8 + row, total[8:16, g * 4 : g * 4 + 1], bias_grad)
    bias_grad_ref[...] = SCALE * jnp.sum(bias_grad, axis=0, keepdims=True)
    for part in (ahead, grad, mixed_in, back_in):
        part.finish()
    narrow_sum.sent()
    wide_sum.sent()
    weight_round.sent()
    sg_copy.wait()
    loop(XL, lambda x: out_copy(x).wait())


VM = pl.BlockSpec(memory_space=pltpu.VMEM)
HB = pl.BlockSpec(memory_space=pl.ANY)
FIELD = (XL, YL, C, NZ)


def local(activations, cotangent, point_weight, bias, spectral_weight):
    tabs = {name: jnp.asarray(value) for name, value in tables().items()}
    scratch = dict(
        act=pltpu.VMEM(FIELD, BF16),
        cot=pltpu.VMEM(FIELD, BF16),
        pre=pltpu.VMEM(FIELD, BF16),
        out=pltpu.VMEM(FIELD, BF16),
        point=pltpu.VMEM(FIELD, F32),
        field=pltpu.VMEM((YL, 4, 8, NZ), F32),
        d=pltpu.VMEM((256, 128), F32),
        rh=pltpu.VMEM((64 * XC, 1024), BF16),
        rl=pltpu.VMEM((64 * XC, 1024), BF16),
        s=pltpu.VMEM((XC * 256, 128), F32),
        yf=pltpu.VMEM((2, 32 * XC, 64 * XC), BF16),
        yi=pltpu.VMEM((2, 32 * XC, 64 * XC), BF16),
        mix=pltpu.VMEM((256, 256), BF16),
        mix_back=pltpu.VMEM((256, 256), BF16),
        weight=pltpu.VMEM((2, KY, 8, 2, C, C), BF16),
        sg=pltpu.VMEM((2, KY, 8, 2, C, C), F32),
        ws=pltpu.VMEM((WIDE, 4, 8, 128), F32),
        wr=pltpu.VMEM((WIDE, 4, 8, 128), F32),
        pg=pltpu.VMEM((256, 256), F32),
        bs=pltpu.VMEM((8, 128), F32),
        ps=pltpu.VMEM((16, 128), F32),
        pr=pltpu.VMEM((NARROW, 16, 128), F32),
        ts=pltpu.VMEM((16, 128), F32),
        tr=pltpu.VMEM((WIDE, 16, 128), F32),
        act_sem=pltpu.SemaphoreType.DMA((XL,)),
        cot_sem=pltpu.SemaphoreType.DMA((XL,)),
        out_sem=pltpu.SemaphoreType.DMA((XL,)),
        table_sem=pltpu.SemaphoreType.DMA((4,)),
        wsem=pltpu.SemaphoreType.DMA((2,)),
        psem=pltpu.SemaphoreType.DMA((2,)),
        tsem=pltpu.SemaphoreType.DMA((2,)),
    )
    for prefix, group in (("f1_", FORWARD), ("f2_", FORWARD), ("i1_", INVERSE), ("i2_", INVERSE)):
        scratch.update({prefix + key: value for key, value in group.items()})
    input_grad, point_grad, bias_grad, spectral_grad = pl.pallas_call(
        functools.partial(kernel, tuple(scratch)),
        name="layer_backward",
        in_specs=[HB, HB, VM, VM, HB, HB, HB, VM, VM, VM, VM, VM, VM, VM],
        out_specs=[HB, VM, VM, HB],
        out_shape=[
            jax.ShapeDtypeStruct(FIELD, BF16),
            jax.ShapeDtypeStruct((C, C), F32),
            jax.ShapeDtypeStruct((1, C), F32),
            jax.ShapeDtypeStruct((2, 1, KY, 8, 2, C, C), F32),
        ],
        scratch_shapes=tuple(scratch.values()),
        compiler_params=pltpu.CompilerParams(
            collective_id=0, has_side_effects=True, vmem_limit_bytes=56 * 1024 * 1024
        ),
    )(
        activations,
        cotangent,
        point_weight,
        bias[None],
        spectral_weight.reshape(2, 1, KY, 8, 2, C, C),
        *(tabs[name] for name in ("yf", "yi", "xf", "xi", "zf", "ziw", "zi1", "pick_c", "pick_o")),
    )

    spectral_grad = spectral_grad.reshape(2, 1, KY, M, C, C)
    return (input_grad, point_grad, bias_grad.reshape(C), spectral_grad)


def solution(mesh):
    return jax.shard_map(
        local,
        mesh=mesh,
        in_specs=(
            P("wide", "narrow", None, None),
            P("wide", "narrow", None, None),
            P(),
            P(),
            P(None, "wide", "narrow", None, None, None),
        ),
        out_specs=(
            P("wide", "narrow", None, None),
            P(),
            P(),
            P(None, "wide", "narrow", None, None, None),
        ),
        check_vma=False,
    )
```

```python
import functools
import math

import jax
import jax.numpy as jnp
import ml_dtypes
import numpy as np
from jax import lax
from jax.experimental import pallas as pl
from jax.experimental.pallas import tpu as pltpu
from jax.sharding import PartitionSpec as P

WIDE = 32
NARROW = 8
M = 16
C = 32
NZ = 256
XL = 8
YL = 32
KY = 4
XC = 2
CHUNKS = XL // XC
ROWS = KY * XC
SCALE = 1.0 / 4096.0

F32 = jnp.float32
BF16 = jnp.bfloat16


def kept(j):
    return np.where(j < 16, j, 224 + j)


def trig(freqs, cells):
    angle = (np.outer(freqs, cells) % 256) * (2.0 * math.pi / 256.0)
    return np.cos(angle), np.sin(angle)


def split_np(table):
    hi = table.astype(np.float32).astype(ml_dtypes.bfloat16)
    lo = (table - hi.astype(np.float64)).astype(np.float32).astype(ml_dtypes.bfloat16)
    return hi, lo


@functools.lru_cache(maxsize=None)
def tables():
    freqs = kept(np.arange(32))
    cos_a, sin_a = trig(freqs, np.arange(256))
    cos_z, sin_z = trig(np.arange(M), np.arange(NZ))
    eye_x = np.eye(XC)
    cy = cos_a.reshape(NARROW, KY, NARROW, YL)
    sy = sin_a.reshape(NARROW, KY, NARROW, YL)
    both = np.stack((cy, sy))
    yf = np.einsum("dtkny,xu->ntkxudy", both, eye_x).reshape(NARROW, 32 * XC, 64 * XC)
    both = np.stack((cy, -sy))
    yi = np.einsum("dtkny,xu->nxydtku", both, eye_x).reshape(NARROW, 32 * XC, 64 * XC)
    xf = np.concatenate((cos_a, sin_a), axis=1) * SCALE
    xi = np.concatenate((cos_a.T, -sin_a.T), axis=1)
    parts = np.stack((cos_z, -sin_z)).reshape(2, 8, 2, NZ)
    zf = np.broadcast_to(parts.transpose(3, 1, 0, 2)[:, :, None], (NZ, 8, 4, 2, 2)).reshape(NZ, 128)
    depth = np.where(np.arange(M) == 0, 1.0, 2.0)[:, None]

    def inverse_z(weights):
        one = (parts * weights.reshape(1, 8, 2, 1)).transpose(1, 0, 2, 3) * SCALE
        full = np.zeros((4, 8, 4, 2, 2, NZ))
        for g in range(4):
            full[g, :, g] = one
        hi, lo = split_np(full.reshape(4, 128, NZ))
        return np.concatenate((hi, hi, lo), axis=1)

    eye = np.eye
    pick_c = np.einsum(
        "gG,pP,kK,co->cgpkPKGo", eye(4), eye(2), eye(2), np.ones((8, C))
    ).reshape(128, 512)
    pick_o = np.einsum(
        "hgo,pP,kK,G->hgpkPKGo", eye(C).reshape(4, 8, C).transpose(1, 0, 2), eye(2), eye(2), np.ones(4)
    ).reshape(128, 512)
    return dict(
        yf=np.stack(split_np(yf), axis=1),
        yi=np.stack(split_np(yi), axis=1),
        xf=np.stack(split_np(xf)),
        xi=np.stack(split_np(xi)),
        zf=np.concatenate(split_np(zf), axis=1),
        ziw=inverse_z(depth),
        zi1=inverse_z(np.ones((M, 1))),
        pick_c=pick_c.astype(ml_dtypes.bfloat16),
        pick_o=pick_o.astype(ml_dtypes.bfloat16),
    )


def dot(a, b):
    return jnp.dot(a, b, preferred_element_type=F32)


def dot_t(a, b):
    return lax.dot_general(a, b, (((1,), (1,)), ((), ())), preferred_element_type=F32)


def halves(x):
    hi = x.astype(BF16)
    return hi, (x - hi.astype(F32)).astype(BF16)


def dot3(table, hi, lo):
    t_hi, t_lo = table[0], table[1]
    return dot(t_hi, hi) + (dot(t_hi, lo) + dot(t_lo, hi))


def lane_of(shape):
    return lax.broadcasted_iota(jnp.int32, shape, len(shape) - 1)


def turn(x):
    real = lax.rem(lane_of(x.shape), 4) < 2
    return jnp.where(real, pltpu.roll(x, 126, x.ndim - 1), -pltpu.roll(x, 2, x.ndim - 1))


def exchange(tiles):
    tiles = list(tiles)
    group = lane_of(tiles[0].shape) // 16
    for step in (1, 2, 4):
        high = lax.rem(group // step, 2) == 1
        for t in range(8):
            if t & step == 0:
                one, two = tiles[t], tiles[t + step]
                tiles[t] = jnp.where(high, pltpu.roll(two, 16 * step, 1), one)
                tiles[t + step] = jnp.where(high, two, pltpu.roll(one, 128 - 16 * step, 1))
    return tiles


def remote(src, dst, send, recv, device):
    return pltpu.make_async_remote_copy(
        src_ref=src,
        dst_ref=dst,
        send_sem=send,
        recv_sem=recv,
        device_id=device,
        device_id_type=pl.DeviceIdType.MESH,
    )


def others(me, size, fn):
    def body(k, carry):
        fn(lax.rem(me + k, size))
        return carry

    lax.fori_loop(1, size, body, 0)


def far_first(me, size, fn):
    x, z, core = me // 16, lax.rem(me // 2, 8), lax.rem(me, 2)

    def body(j, carry):
        i, sub = j // 4, lax.rem(j, 4)
        dz = 4 + (1 - 2 * lax.rem(i, 2)) * ((i + 1) // 2)
        dx, dcore = 1 - sub // 2, 1 - lax.rem(sub, 2)
        fn(lax.rem(x + dx, 2) * 16 + lax.rem(z + dz, 8) * 2 + lax.rem(core + dcore, 2))
        return carry

    lax.fori_loop(0, size - 1, body, 0)


def greet(n, w):
    barrier = pltpu.get_barrier_semaphore()

    def signal(axis):
        return lambda t: pl.semaphore_signal(
            barrier, inc=1, device_id={axis: t}, device_id_type=pl.DeviceIdType.MESH
        )

    others(n, NARROW, signal("narrow"))
    others(w, WIDE, signal("wide"))
    return barrier


def greeted(barrier):
    pl.semaphore_wait(barrier, NARROW + WIDE - 2)


def loop(count, fn):
    def body(i, carry):
        fn(i)
        return carry

    lax.fori_loop(0, count, body, 0)


class Names:
    def __init__(self, names, refs):
        for name, ref in zip(names, refs):
            setattr(self, name, ref)


class Round:
    def __init__(self, axis, size, me, src, dst, send, recv):
        self.axis, self.size, self.me = axis, size, me
        self.src, self.dst, self.send, self.recv = src, dst, send, recv

    def start(self, whole=False):
        order = far_first if self.size == WIDE else others

        def one(t):
            remote(
                self.src if whole else self.src.at[t],
                self.dst.at[self.me],
                self.send,
                self.recv,
                {self.axis: t},
            ).start()

        order(self.me, self.size, one)

    def all_of(self):
        part = self.dst.at[pl.ds(0, self.size - 1)]
        return remote(part, part, self.send, self.recv, {self.axis: lax.rem(self.me + 1, self.size)})

    def arrived(self):
        self.all_of().wait_recv()

    def sent(self):
        self.all_of().wait_send()


FORWARD = dict(
    ys=pltpu.VMEM((CHUNKS, NARROW, ROWS, 1024), F32),
    yr=pltpu.VMEM((CHUNKS, NARROW, ROWS, 1024), F32),
    xs=pltpu.VMEM((WIDE, 8, 128), F32),
    xr=pltpu.VMEM((WIDE, 8, 128), F32),
    ms=pltpu.VMEM((WIDE, 1, 128), F32),
    mr=pltpu.VMEM((WIDE, 1, 128), F32),
    ysem=pltpu.SemaphoreType.DMA((2, CHUNKS)),
    xsem=pltpu.SemaphoreType.DMA((2,)),
    msem=pltpu.SemaphoreType.DMA((2,)),
)

INVERSE = dict(
    vs=pltpu.VMEM((WIDE, 8, 128), F32),
    vr=pltpu.VMEM((WIDE, 8, 128), F32),
    as_=pltpu.VMEM((CHUNKS, ROWS, 1024), F32),
    ar=pltpu.VMEM((CHUNKS, NARROW, ROWS, 1024), F32),
    vsem=pltpu.SemaphoreType.DMA((2,)),
    asem=pltpu.SemaphoreType.DMA((2, CHUNKS)),
)


def depth_forward(field, zf):
    full = dot(field.reshape(YL * C, NZ), zf)
    full = (full[:, :128] + full[:, 128:]).reshape(YL, 4, 8, 128)
    group = lax.rem(lane_of((YL, 8, 128)) // 4, 4)
    low = jnp.where(group == 0, full[:, 0], full[:, 1])
    high = jnp.where(group == 2, full[:, 2], full[:, 3])
    return jnp.where(group < 2, low, high)


class Forward:
    def __init__(self, s, own, n, w):
        self.s, self.own, self.n, self.w = s, own, n, w
        self.x = Round("wide", WIDE, w, own.xs, own.xr, own.xsem.at[0], own.xsem.at[1])
        self.m = Round("wide", WIDE, w, own.ms, own.mr, own.msem.at[0], own.msem.at[1])

    def y(self, q):
        o = self.own
        return Round("narrow", NARROW, self.n, o.ys.at[q], o.yr.at[q], o.ysem.at[0, q], o.ysem.at[1, q])

    def put_rows(self, i, depth):
        s = self.s
        s.d[...] = depth.reshape(YL * 8, 128)
        rows = pl.multiple_of(i * 64, 64)
        turned = pl.multiple_of(i * 64 + 32, 32)
        for c8 in range(8):
            part = s.d[pl.ds(c8, YL, stride=8), :]
            lanes = slice(c8 * 128, c8 * 128 + 128)
            s.rh[pl.ds(rows, 32), lanes], s.rl[pl.ds(rows, 32), lanes] = halves(part)
            s.rh[pl.ds(turned, 32), lanes], s.rl[pl.ds(turned, 32), lanes] = halves(turn(part))

    def send_chunk(self, q):
        s, o = self.s, self.own
        out = dot3(s.yf, s.rh[...], s.rl[...])
        o.ys[q] = out.reshape(NARROW, ROWS, 1024)
        o.yr[q, self.n] = o.ys[q, self.n]
        self.y(q).start()

    def sum_chunks(self):
        o = self.own
        for q in range(CHUNKS):
            self.y(q).arrived()
            total = o.yr[q, 0]
            for t in range(1, NARROW):
                total = total + o.yr[q, t]
            tiles = exchange([total[:, t * 128 : t * 128 + 128] for t in range(8)])
            for k in range(KY):
                for t in range(8):
                    o.xs[k * 8 + t, q * XC : q * XC + XC] = tiles[t][k * XC : k * XC + XC]
        o.xr[self.w] = o.xs[self.w]
        self.x.start()

    def modes(self, xf):
        o = self.own
        self.x.arrived()
        cells = o.xr[...].reshape(256, 128)
        hi, lo = halves(jnp.concatenate((cells, turn(cells)), axis=0))
        return dot3(xf, hi, lo)

    def to_owner(self, modes):
        o = self.own
        o.ms[...] = modes.reshape(WIDE, 1, 128)
        o.mr[self.w] = o.ms[self.w]
        self.m.start()

    def owned(self):
        self.m.arrived()
        return self.own.mr[...].reshape(WIDE, 128)

    def finish(self):
        loop(CHUNKS, lambda q: self.y(q).sent())
        self.x.sent()
        self.m.sent()


class Inverse:
    def __init__(self, s, own, n, w):
        self.s, self.own, self.n, self.w = s, own, n, w
        self.x = Round("wide", WIDE, w, own.vs, own.vr, own.vsem.at[0], own.vsem.at[1])

    def y(self, q):
        o = self.own
        return Round("narrow", NARROW, self.n, o.as_.at[q], o.ar.at[q], o.asem.at[0, q], o.asem.at[1, q])

    def to_cells(self, modes, xi):
        o = self.own
        hi, lo = halves(jnp.concatenate((modes, turn(modes)), axis=0))
        o.vs[...] = dot3(xi, hi, lo).reshape(WIDE, 8, 128)
        o.vr[self.w] = o.vs[self.w]
        self.x.start()

    def gather(self):
        o = self.own
        self.x.arrived()
        tiles = [exchange([o.vr[k * 8 + t] for t in range(8)]) for k in range(KY)]
        for q in range(CHUNKS):
            for k in range(KY):
                for c8 in range(8):
                    o.as_[q, k * XC : k * XC + XC, c8 * 128 : c8 * 128 + 128] = tiles[k][c8][
                        q * XC : q * XC + XC
                    ]
            o.ar[q, self.n] = o.as_[q]
            self.y(q).start(whole=True)

    def chunk(self, q):
        s, o = self.s, self.own
        self.y(q).arrived()
        columns = []
        for c8 in range(8):
            part = o.ar[q, :, :, c8 * 128 : c8 * 128 + 128].reshape(NARROW * ROWS, 128)
            columns.append(jnp.concatenate((part, turn(part)), axis=0))
        hi, lo = halves(jnp.concatenate(columns, axis=1))
        out = dot3(s.yi, hi, lo)
        for i in range(XC):
            for c8 in range(8):
                s.s[pl.ds(i * 256 + c8, YL, stride=8), :] = out[
                    i * YL : i * YL + YL, c8 * 128 : c8 * 128 + 128
                ]

    def field_row(self, i, zi):
        s = self.s
        hi, lo = halves(s.s[pl.ds(pl.multiple_of(i * 256, 256), 256), :])
        both = jnp.concatenate((hi, lo, hi), axis=1)
        for g in range(4):
            s.field[:, g] = dot(both, zi[g]).reshape(YL, 8, NZ)

    def finish(self):
        self.x.sent()
        loop(CHUNKS, lambda q: self.y(q).sent())


def fold_point(full):
    row = lax.broadcasted_iota(jnp.int32, full.shape, 0) // 32
    full = jnp.where(row == lane_of(full.shape) // 32, full, 0.0)
    total = full[0:32]
    for y in range(1, 8):
        total = total + full[y * 32 : y * 32 + 32]
    total = total[:, :128] + total[:, 128:]
    total = total + pltpu.roll(total, 64, 1)
    total = total + pltpu.roll(total, 32, 1)
    lane = lane_of((8, 128))
    low = jnp.where(lane < 32, total[0:8], total[8:16])
    high = jnp.where(lane < 96, total[16:24], total[24:32])
    return jnp.where(lane < 64, low, high)


def gelu_slope(u):
    k = math.sqrt(2.0 / math.pi)
    square = u * u
    h = 0.5 * jnp.tanh(u * (k + (k * 0.044715) * square)) + 0.5
    return h + h * (1.0 - h) * (u * (2.0 * k + (6.0 * k * 0.044715) * square))


def select(rows, pick):
    hi, lo = halves(rows)
    return dot(hi, pick) + dot(lo, pick)


def gather_back(columns, pick):
    hi, lo = halves(columns)
    return dot_t(hi, pick) + dot_t(lo, pick)


def part_of(columns, part, k2):
    at = (2 * part + k2) * 128
    return columns[:, at : at + 128]


def own_channel(rows):
    row = lax.rem(lax.broadcasted_iota(jnp.int32, rows.shape, 0), 8)
    return jnp.where(lane_of(rows.shape) // 16 == row, rows, 0.0)


def over_rows(rows):
    lanes = rows.shape[1]
    return jnp.broadcast_to(rows[:, None], (WIDE, 8, lanes)).reshape(WIDE * 8, lanes)


def by_input(modes, pick_c):
    return select(own_channel(over_rows(modes)), pick_c)


def weight_of(wr):
    def at(part, k2):
        return wr[:, 2 * part + k2].reshape(WIDE * 8, 128)

    return at


def mix_modes(modes, weight, pick_c, pick_o):
    columns = by_input(modes, pick_c)
    real, imag = [], []
    for k2 in range(2):
        c_real, c_imag = part_of(columns, 0, k2), part_of(columns, 1, k2)
        w_real, w_imag = weight(0, k2), weight(1, k2)
        real.append(c_real * w_real - c_imag * w_imag)
        imag.append(c_real * w_imag + c_imag * w_real)
    full = jnp.concatenate(real + imag, axis=1).reshape(WIDE, 8, 512)
    return gather_back(jnp.sum(full, axis=1), pick_o)


def mix_back(grads, weight, pick_c, pick_o):
    columns = over_rows(select(grads, pick_o))
    real, imag = [], []
    for k2 in range(2):
        g_real, g_imag = part_of(columns, 0, k2), part_of(columns, 1, k2)
        w_real, w_imag = weight(0, k2), weight(1, k2)
        real.append(g_real * w_real + g_imag * w_imag)
        imag.append(g_imag * w_real - g_real * w_imag)
    full = own_channel(gather_back(jnp.concatenate(real + imag, axis=1), pick_c))
    return jnp.sum(full.reshape(WIDE, 8, 128), axis=1)


def outer_modes(sg_ref, modes, grads, pick_c, pick_o):
    first = by_input(modes, pick_c)
    second = over_rows(select(grads, pick_o))
    for k2 in range(2):
        c_real, c_imag = part_of(first, 0, k2), part_of(first, 1, k2)
        g_real, g_imag = part_of(second, 0, k2), part_of(second, 1, k2)
        for part, value in enumerate(
            (c_real * g_real + c_imag * g_imag, c_real * g_imag - c_imag * g_real)
        ):
            for g in range(4):
                moved = pltpu.roll(value, (128 - 32 * g) % 128, 1) if g else value
                sg_ref[part, 0, :, :, k2, g * 8 : g * 8 + 8, :] = moved[:, :C].reshape(KY, 8, 8, C)


def pack_weight(s, n, w):
    def one(k):
        for part in range(2):
            for k2 in range(2):
                full = s.weight[part, k, :, k2].astype(F32)
                tile = jnp.concatenate([full[:, g * 8 : g * 8 + 8] for g in range(4)], axis=-1)
                s.ws[pl.ds(pl.multiple_of(k * 8, 8), 8), 2 * part + k2] = tile

    loop(KY, one)
    s.wr[w] = s.ws[w]


def kernel(
    names,
    act_hbm,
    cot_hbm,
    point_ref,
    bias_ref,
    weight_hbm,
    yf_hbm,
    yi_hbm,
    xf_ref,
    xi_ref,
    zf_ref,
    ziw_ref,
    zi1_ref,
    pick_c_ref,
    pick_o_ref,
    out_ref,
    point_grad_ref,
    bias_grad_ref,
    sg_ref,
    *refs,
):
    s = Names(names, refs)
    n, w = lax.axis_index("narrow"), lax.axis_index("wide")

    def group(prefix, keys):
        keys = tuple(keys)
        return Names(keys, [getattr(s, prefix + key) for key in keys])

    ahead = Forward(s, group("f1_", FORWARD), n, w)
    grad = Forward(s, group("f2_", FORWARD), n, w)
    mixed_in = Inverse(s, group("i1_", INVERSE), n, w)
    back_in = Inverse(s, group("i2_", INVERSE), n, w)

    def act_copy(x):
        return pltpu.make_async_copy(act_hbm.at[x], s.act.at[x], s.act_sem.at[x])

    def cot_copy(x):
        return pltpu.make_async_copy(cot_hbm.at[x], s.cot.at[x], s.cot_sem.at[x])

    table_in = [
        pltpu.make_async_copy(yf_hbm.at[n], s.yf, s.table_sem.at[0]),
        pltpu.make_async_copy(yi_hbm.at[n], s.yi, s.table_sem.at[1]),
    ]
    weight_copy = pltpu.make_async_copy(weight_hbm.at[:, 0], s.weight, s.table_sem.at[2])
    weight_copy.start()
    barrier = greet(n, w)
    for copy in table_in:
        copy.start()
    loop(XL, lambda x: act_copy(x).start())
    loop(XL, lambda x: cot_copy(x).start())
    weight_round = Round("wide", WIDE, w, s.ws, s.wr, s.wsem.at[0], s.wsem.at[1])
    weight_copy.wait()
    pack_weight(s, n, w)
    for copy in table_in:
        copy.wait()

    def forward_chunk(q):
        def row(i):
            x = q * XC + i
            act_copy(x).wait()
            ahead.put_rows(i, depth_forward(s.act[x], zf_ref[...]))

        loop(XC, row)

        @pl.when(q == 0)
        def _():
            greeted(barrier)

        ahead.send_chunk(q)

        @pl.when(q == 0)
        def _():
            weight_round.start()

    loop(CHUNKS, forward_chunk)

    row = lax.broadcasted_iota(jnp.int32, (256, 32), 0)
    pick = lax.rem(row, 32) == lane_of((256, 32))
    ones = jnp.where(pick, 1.0, 0.0).astype(BF16)
    bias_rows = jnp.sum(jnp.where(pick, bias_ref[...], 0.0), axis=1, keepdims=True)
    same = lax.broadcasted_iota(jnp.int32, (256, 256), 0) // 32 == lane_of((256, 256)) // 32
    tall = dot(ones, point_ref[...]).astype(BF16)
    s.mix_back[...] = jnp.where(same, dot_t(tall, ones), 0.0).astype(BF16)
    tall = dot_t(ones, point_ref[...]).astype(BF16)
    s.mix[...] = jnp.where(same, dot_t(tall, ones), 0.0).astype(BF16)

    def blocks(fn, low, high):
        def one(i, carry):
            fn(i // 4, pl.ds(pl.multiple_of(lax.rem(i, 4) * 8, 8), 8))
            return carry

        lax.fori_loop(low, high, one, 0)

    def mix_block(x, ys):
        point = dot(s.mix[...], s.act[x, ys].reshape(256, NZ)) + bias_rows
        s.point[x, ys] = point.reshape(8, C, NZ)

    pick_c, pick_o = pick_c_ref[...], pick_o_ref[...]
    weight = weight_of(s.wr)
    blocks(mix_block, 0, 20)
    ahead.sum_chunks()
    blocks(mix_block, 20, 26)
    weight_round.arrived()
    coeffs = ahead.modes(xf_ref)
    mixed_in.to_cells(mix_modes(coeffs, weight, pick_c, pick_o), xi_ref)
    ahead.to_owner(coeffs)
    s.bs[...] = jnp.zeros_like(s.bs)
    s.pg[...] = jnp.zeros_like(s.pg)
    blocks(mix_block, 26, 4 * XL)
    mixed_in.gather()

    def middle_chunk(q):
        mixed_in.chunk(q)

        def row(i):
            x = q * XC + i
            cot_copy(x).wait()
            mixed_in.field_row(i, ziw_ref)

            def block(b):
                ys = pl.ds(pl.multiple_of(b * 8, 8), 8)
                preact = s.field[ys].reshape(256, NZ) + s.point[x, ys].reshape(256, NZ)
                cot = s.cot[x, ys].reshape(256, NZ).astype(F32)
                pre = (cot * gelu_slope(preact)).astype(BF16)
                s.pre[x, ys] = pre.reshape(8, C, NZ)

            loop(4, block)
            depth = depth_forward(s.pre[x], zf_ref[...])
            s.bs[...] += jnp.sum(depth, axis=0)
            grad.put_rows(i, depth)

        loop(XC, row)
        grad.send_chunk(q)

    loop(CHUNKS, middle_chunk)

    def back_block(x, ys):
        pre = s.pre[x, ys].reshape(256, NZ)
        s.pg[...] += dot_t(s.act[x, ys].reshape(256, NZ), pre)
        s.point[x, ys] = dot(s.mix_back[...], pre).reshape(8, C, NZ)

    blocks(back_block, 0, 8)
    grad.sum_chunks()
    blocks(back_block, 8, 20)
    rows = grad.modes(xf_ref)
    first = lax.rem(w, 8) == 0
    grads = rows * jnp.where((lax.rem(lane_of(rows.shape), 2) == 0) & first, 1.0, 2.0)
    back_in.to_cells(mix_back(grads, weight, pick_c, pick_o), xi_ref)
    grad.to_owner(grads)
    blocks(back_block, 20, 4 * XL)
    s.ps[0:8] = fold_point(s.pg[...])
    s.ps[8:16] = s.bs[...]
    s.pr[n] = s.ps[...]
    narrow_sum = Round("narrow", NARROW, n, s.ps, s.pr, s.psem.at[0], s.psem.at[1])
    narrow_sum.start(whole=True)
    back_in.gather()
    outer_modes(sg_ref, ahead.owned(), grad.owned(), pick_c, pick_o)
    narrow_sum.arrived()
    total = s.pr[0]
    for t in range(1, NARROW):
        total = total + s.pr[t]
    s.ts[...] = total
    s.tr[w] = total
    wide_sum = Round("wide", WIDE, w, s.ts, s.tr, s.tsem.at[0], s.tsem.at[1])
    wide_sum.start(whole=True)

    def last_chunk(q):
        back_in.chunk(q)

        def row(i):
            x = q * XC + i
            back_in.field_row(i, zi1_ref)

            def block(b):
                ys = pl.ds(pl.multiple_of(b * 8, 8), 8)
                out = s.field[ys].reshape(256, NZ) + s.point[x, ys].reshape(256, NZ)
                out_ref[x, ys] = out.astype(BF16).reshape(8, C, NZ)

            loop(4, block)

        loop(XC, row)

    loop(CHUNKS, last_chunk)
    wide_sum.arrived()
    total = s.tr[0]
    for t in range(1, WIDE):
        total = total + s.tr[t]
    for g in range(4):
        point_grad_ref[g * 8 : g * 8 + 8] = SCALE * total[0:8, g * 32 : g * 32 + C]
    row, lane = lax.broadcasted_iota(jnp.int32, (8, C), 0), lane_of((8, C))
    bias_grad = jnp.zeros((8, C), F32)
    for g in range(4):
        bias_grad = jnp.where(lane == g * 8 + row, total[8:16, g * 4 : g * 4 + 1], bias_grad)
    bias_grad_ref[...] = SCALE * jnp.sum(bias_grad, axis=0, keepdims=True)
    for part in (ahead, grad, mixed_in, back_in):
        part.finish()
    narrow_sum.sent()
    wide_sum.sent()
    weight_round.sent()


def write_kernel(*refs):
    sources, targets, sems = refs[:4], refs[4:8], refs[8]
    copies = [
        pltpu.make_async_copy(sources[0].at[x], targets[0].at[x], sems.at[x]) for x in range(XL)
    ] + [
        pltpu.make_async_copy(source, target, sems.at[XL + i])
        for i, (source, target) in enumerate(zip(sources[1:], targets[1:]))
    ]
    for copy in copies:
        copy.start()
    for copy in copies:
        copy.wait()


def write_out(*arrays):
    return pl.pallas_call(
        write_kernel,
        name="write_results",
        in_specs=[VM] * 4,
        out_specs=[HB] * 4,
        out_shape=[jax.ShapeDtypeStruct(a.shape, a.dtype) for a in arrays],
        scratch_shapes=[pltpu.SemaphoreType.DMA((XL + 3,))],
        compiler_params=pltpu.CompilerParams(vmem_limit_bytes=1024 * 1024),
    )(*arrays)


VM = pl.BlockSpec(memory_space=pltpu.VMEM)
HB = pl.BlockSpec(memory_space=pl.ANY)
FIELD = (XL, YL, C, NZ)


def local(activations, cotangent, point_weight, bias, spectral_weight):
    tabs = {name: jnp.asarray(value) for name, value in tables().items()}
    scratch = dict(
        act=pltpu.VMEM(FIELD, BF16),
        cot=pltpu.VMEM(FIELD, BF16),
        pre=pltpu.VMEM(FIELD, BF16),
        point=pltpu.VMEM(FIELD, F32),
        field=pltpu.VMEM((YL, 4, 8, NZ), F32),
        d=pltpu.VMEM((256, 128), F32),
        rh=pltpu.VMEM((64 * XC, 1024), BF16),
        rl=pltpu.VMEM((64 * XC, 1024), BF16),
        s=pltpu.VMEM((XC * 256, 128), F32),
        yf=pltpu.VMEM((2, 32 * XC, 64 * XC), BF16),
        yi=pltpu.VMEM((2, 32 * XC, 64 * XC), BF16),
        mix=pltpu.VMEM((256, 256), BF16),
        mix_back=pltpu.VMEM((256, 256), BF16),
        weight=pltpu.VMEM((2, KY, 8, 2, C, C), BF16),
        ws=pltpu.VMEM((WIDE, 4, 8, 128), F32),
        wr=pltpu.VMEM((WIDE, 4, 8, 128), F32),
        pg=pltpu.VMEM((256, 256), F32),
        bs=pltpu.VMEM((8, 128), F32),
        ps=pltpu.VMEM((16, 128), F32),
        pr=pltpu.VMEM((NARROW, 16, 128), F32),
        ts=pltpu.VMEM((16, 128), F32),
        tr=pltpu.VMEM((WIDE, 16, 128), F32),
        act_sem=pltpu.SemaphoreType.DMA((XL,)),
        cot_sem=pltpu.SemaphoreType.DMA((XL,)),
        table_sem=pltpu.SemaphoreType.DMA((4,)),
        wsem=pltpu.SemaphoreType.DMA((2,)),
        psem=pltpu.SemaphoreType.DMA((2,)),
        tsem=pltpu.SemaphoreType.DMA((2,)),
    )
    for prefix, group in (("f1_", FORWARD), ("f2_", FORWARD), ("i1_", INVERSE), ("i2_", INVERSE)):
        scratch.update({prefix + key: value for key, value in group.items()})
    input_grad, point_grad, bias_grad, spectral_grad = pl.pallas_call(
        functools.partial(kernel, tuple(scratch)),
        name="layer_backward",
        in_specs=[HB, HB, VM, VM, HB, HB, HB, VM, VM, VM, VM, VM, VM, VM],
        out_specs=[VM, VM, VM, VM],
        out_shape=[
            pltpu.VMEM(FIELD, BF16),
            pltpu.VMEM((C, C), F32),
            pltpu.VMEM((1, C), F32),
            pltpu.VMEM((2, 1, KY, 8, 2, C, C), F32),
        ],
        scratch_shapes=tuple(scratch.values()),
        compiler_params=pltpu.CompilerParams(
            collective_id=0, has_side_effects=True, vmem_limit_bytes=48 * 1024 * 1024
        ),
    )(
        activations,
        cotangent,
        point_weight,
        bias[None],
        spectral_weight.reshape(2, 1, KY, 8, 2, C, C),
        *(tabs[name] for name in ("yf", "yi", "xf", "xi", "zf", "ziw", "zi1", "pick_c", "pick_o")),
    )

    input_grad, point_grad, bias_grad, spectral_grad = write_out(
        input_grad, point_grad, bias_grad, spectral_grad
    )
    spectral_grad = spectral_grad.reshape(2, 1, KY, M, C, C)
    return (input_grad, point_grad, bias_grad.reshape(C), spectral_grad)


def solution(mesh):
    return jax.shard_map(
        local,
        mesh=mesh,
        in_specs=(
            P("wide", "narrow", None, None),
            P("wide", "narrow", None, None),
            P(),
            P(),
            P(None, "wide", "narrow", None, None, None),
        ),
        out_specs=(
            P("wide", "narrow", None, None),
            P(),
            P(),
            P(None, "wide", "narrow", None, None, None),
        ),
        check_vma=False,
    )
```

```python
import functools
import math

import jax
import jax.numpy as jnp
import ml_dtypes
import numpy as np
from jax import lax
from jax.experimental import pallas as pl
from jax.experimental.pallas import tpu as pltpu
from jax.sharding import PartitionSpec as P

WIDE = 32
NARROW = 8
M = 16
C = 32
NZ = 256
XL = 8
YL = 32
KY = 4
XC = 2
CHUNKS = XL // XC
ROWS = KY * XC
SCALE = 1.0 / 4096.0

F32 = jnp.float32
BF16 = jnp.bfloat16


def kept(j):
    return np.where(j < 16, j, 224 + j)


def trig(freqs, cells):
    angle = (np.outer(freqs, cells) % 256) * (2.0 * math.pi / 256.0)
    return np.cos(angle), np.sin(angle)


def split_np(table):
    hi = table.astype(np.float32).astype(ml_dtypes.bfloat16)
    lo = (table - hi.astype(np.float64)).astype(np.float32).astype(ml_dtypes.bfloat16)
    return hi, lo


@functools.lru_cache(maxsize=None)
def tables():
    freqs = kept(np.arange(32))
    cos_a, sin_a = trig(freqs, np.arange(256))
    cos_z, sin_z = trig(np.arange(M), np.arange(NZ))
    eye_x = np.eye(XC)
    cy = cos_a.reshape(NARROW, KY, NARROW, YL)
    sy = sin_a.reshape(NARROW, KY, NARROW, YL)
    both = np.stack((cy, sy))
    yf = np.einsum("dtkny,xu->ntkxudy", both, eye_x).reshape(NARROW, 32 * XC, 64 * XC)
    both = np.stack((cy, -sy))
    yi = np.einsum("dtkny,xu->nxydtku", both, eye_x).reshape(NARROW, 32 * XC, 64 * XC)
    xf = np.concatenate((cos_a, sin_a), axis=1) * SCALE
    xi = np.concatenate((cos_a.T, -sin_a.T), axis=1)
    parts = np.stack((cos_z, -sin_z)).reshape(2, 8, 2, NZ)
    zf = np.broadcast_to(parts.transpose(3, 1, 0, 2)[:, :, None], (NZ, 8, 4, 2, 2)).reshape(NZ, 128)
    depth = np.where(np.arange(M) == 0, 1.0, 2.0)[:, None]

    def inverse_z(weights):
        one = (parts * weights.reshape(1, 8, 2, 1)).transpose(1, 0, 2, 3) * SCALE
        full = np.zeros((4, 8, 4, 2, 2, NZ))
        for g in range(4):
            full[g, :, g] = one
        hi, lo = split_np(full.reshape(4, 128, NZ))
        return np.concatenate((hi, hi, lo), axis=1)

    eye = np.eye
    pick_c = np.einsum(
        "gG,pP,kK,co->cgpkPKGo", eye(4), eye(2), eye(2), np.ones((8, C))
    ).reshape(128, 512)
    pick_o = np.einsum(
        "hgo,pP,kK,G->hgpkPKGo", eye(C).reshape(4, 8, C).transpose(1, 0, 2), eye(2), eye(2), np.ones(4)
    ).reshape(128, 512)
    return dict(
        yf=np.stack(split_np(yf), axis=1),
        yi=np.stack(split_np(yi), axis=1),
        xf=np.stack(split_np(xf)),
        xi=np.stack(split_np(xi)),
        zf=np.concatenate(split_np(zf), axis=1),
        ziw=inverse_z(depth),
        zi1=inverse_z(np.ones((M, 1))),
        pick_c=pick_c.astype(ml_dtypes.bfloat16),
        pick_o=pick_o.astype(ml_dtypes.bfloat16),
    )


def dot(a, b):
    return jnp.dot(a, b, preferred_element_type=F32)


def dot_t(a, b):
    return lax.dot_general(a, b, (((1,), (1,)), ((), ())), preferred_element_type=F32)


def halves(x):
    hi = x.astype(BF16)
    return hi, (x - hi.astype(F32)).astype(BF16)


def dot3(table, hi, lo):
    t_hi, t_lo = table[0], table[1]
    return dot(t_hi, hi) + (dot(t_hi, lo) + dot(t_lo, hi))


def lane_of(shape):
    return lax.broadcasted_iota(jnp.int32, shape, len(shape) - 1)


def turn(x):
    real = lax.rem(lane_of(x.shape), 4) < 2
    return jnp.where(real, pltpu.roll(x, 126, x.ndim - 1), -pltpu.roll(x, 2, x.ndim - 1))


def exchange(tiles):
    tiles = list(tiles)
    group = lane_of(tiles[0].shape) // 16
    for step in (1, 2, 4):
        high = lax.rem(group // step, 2) == 1
        for t in range(8):
            if t & step == 0:
                one, two = tiles[t], tiles[t + step]
                tiles[t] = jnp.where(high, pltpu.roll(two, 16 * step, 1), one)
                tiles[t + step] = jnp.where(high, two, pltpu.roll(one, 128 - 16 * step, 1))
    return tiles


def remote(src, dst, send, recv, device):
    return pltpu.make_async_remote_copy(
        src_ref=src,
        dst_ref=dst,
        send_sem=send,
        recv_sem=recv,
        device_id=device,
        device_id_type=pl.DeviceIdType.MESH,
    )


def far_first(me, size, fn):
    fast = 4 if size == WIDE else 2
    ring = 8 if size == WIDE else 4
    x, z, last = me // 16, lax.rem(me // 2, ring), lax.rem(me, 2)

    def body(j, carry):
        i, sub = j // fast, lax.rem(j, fast)
        dz = ring // 2 + (1 - 2 * lax.rem(i, 2)) * ((i + 1) // 2)
        to = lax.rem(z + dz, ring) * 2 + lax.rem(last + 1 - lax.rem(sub, 2), 2)
        if size == WIDE:
            to = to + lax.rem(x + 1 - sub // 2, 2) * 16
        fn(to)
        return carry

    lax.fori_loop(0, size - 1, body, 0)


def greet(n, w):
    barrier = pltpu.get_barrier_semaphore()

    def signal(axis):
        return lambda t: pl.semaphore_signal(
            barrier, inc=1, device_id={axis: t}, device_id_type=pl.DeviceIdType.MESH
        )

    far_first(w, WIDE, signal("wide"))
    far_first(n, NARROW, signal("narrow"))
    return barrier


def greeted(barrier):
    pl.semaphore_wait(barrier, NARROW + WIDE - 2)


def loop(count, fn):
    def body(i, carry):
        fn(i)
        return carry

    lax.fori_loop(0, count, body, 0)


class Names:
    def __init__(self, names, refs):
        for name, ref in zip(names, refs):
            setattr(self, name, ref)


class Round:
    def __init__(self, axis, size, me, src, dst, send, recv):
        self.axis, self.size, self.me = axis, size, me
        self.src, self.dst, self.send, self.recv = src, dst, send, recv

    def start(self, whole=False):
        def one(t):
            remote(
                self.src if whole else self.src.at[t],
                self.dst.at[self.me],
                self.send,
                self.recv,
                {self.axis: t},
            ).start()

        far_first(self.me, self.size, one)

    def all_of(self):
        part = self.dst.at[pl.ds(0, self.size - 1)]
        return remote(part, part, self.send, self.recv, {self.axis: lax.rem(self.me + 1, self.size)})

    def arrived(self):
        self.all_of().wait_recv()

    def sent(self):
        self.all_of().wait_send()


FORWARD = dict(
    ys=pltpu.VMEM((CHUNKS, NARROW, ROWS, 1024), F32),
    yr=pltpu.VMEM((CHUNKS, NARROW, ROWS, 1024), F32),
    xs=pltpu.VMEM((WIDE, 8, 128), F32),
    xr=pltpu.VMEM((WIDE, 8, 128), F32),
    ms=pltpu.VMEM((WIDE, 1, 128), F32),
    mr=pltpu.VMEM((WIDE, 1, 128), F32),
    ysem=pltpu.SemaphoreType.DMA((2, CHUNKS)),
    xsem=pltpu.SemaphoreType.DMA((2,)),
    msem=pltpu.SemaphoreType.DMA((2,)),
)

INVERSE = dict(
    vs=pltpu.VMEM((WIDE, 8, 128), F32),
    vr=pltpu.VMEM((WIDE, 8, 128), F32),
    as_=pltpu.VMEM((CHUNKS, ROWS, 1024), F32),
    ar=pltpu.VMEM((CHUNKS, NARROW, ROWS, 1024), F32),
    vsem=pltpu.SemaphoreType.DMA((2,)),
    asem=pltpu.SemaphoreType.DMA((2, CHUNKS)),
)


def depth_forward(field, zf):
    full = dot(field.reshape(YL * C, NZ), zf)
    full = (full[:, :128] + full[:, 128:]).reshape(YL, 4, 8, 128)
    group = lax.rem(lane_of((YL, 8, 128)) // 4, 4)
    low = jnp.where(group == 0, full[:, 0], full[:, 1])
    high = jnp.where(group == 2, full[:, 2], full[:, 3])
    return jnp.where(group < 2, low, high)


class Forward:
    def __init__(self, s, own, n, w):
        self.s, self.own, self.n, self.w = s, own, n, w
        self.x = Round("wide", WIDE, w, own.xs, own.xr, own.xsem.at[0], own.xsem.at[1])
        self.m = Round("wide", WIDE, w, own.ms, own.mr, own.msem.at[0], own.msem.at[1])

    def y(self, q):
        o = self.own
        return Round("narrow", NARROW, self.n, o.ys.at[q], o.yr.at[q], o.ysem.at[0, q], o.ysem.at[1, q])

    def put_rows(self, i, depth):
        s = self.s
        s.d[...] = depth.reshape(YL * 8, 128)
        rows = pl.multiple_of(i * 64, 64)
        turned = pl.multiple_of(i * 64 + 32, 32)
        for c8 in range(8):
            part = s.d[pl.ds(c8, YL, stride=8), :]
            lanes = slice(c8 * 128, c8 * 128 + 128)
            s.rh[pl.ds(rows, 32), lanes], s.rl[pl.ds(rows, 32), lanes] = halves(part)
            s.rh[pl.ds(turned, 32), lanes], s.rl[pl.ds(turned, 32), lanes] = halves(turn(part))

    def send_chunk(self, q):
        s, o = self.s, self.own
        out = dot3(s.yf, s.rh[...], s.rl[...])
        o.ys[q] = out.reshape(NARROW, ROWS, 1024)
        o.yr[q, self.n] = o.ys[q, self.n]
        self.y(q).start()

    def sum_chunks(self):
        o = self.own
        for q in range(CHUNKS):
            self.y(q).arrived()
            total = o.yr[q, 0]
            for t in range(1, NARROW):
                total = total + o.yr[q, t]
            tiles = exchange([total[:, t * 128 : t * 128 + 128] for t in range(8)])
            for k in range(KY):
                for t in range(8):
                    o.xs[k * 8 + t, q * XC : q * XC + XC] = tiles[t][k * XC : k * XC + XC]
        o.xr[self.w] = o.xs[self.w]
        self.x.start()

    def modes(self, xf):
        o = self.own
        self.x.arrived()
        cells = o.xr[...].reshape(256, 128)
        hi, lo = halves(jnp.concatenate((cells, turn(cells)), axis=0))
        return dot3(xf, hi, lo)

    def to_owner(self, modes):
        o = self.own
        o.ms[...] = modes.reshape(WIDE, 1, 128)
        o.mr[self.w] = o.ms[self.w]
        self.m.start()

    def owned(self):
        self.m.arrived()
        return self.own.mr[...].reshape(WIDE, 128)

    def finish(self):
        loop(CHUNKS, lambda q: self.y(q).sent())
        self.x.sent()
        self.m.sent()


class Inverse:
    def __init__(self, s, own, n, w):
        self.s, self.own, self.n, self.w = s, own, n, w
        self.x = Round("wide", WIDE, w, own.vs, own.vr, own.vsem.at[0], own.vsem.at[1])

    def y(self, q):
        o = self.own
        return Round("narrow", NARROW, self.n, o.as_.at[q], o.ar.at[q], o.asem.at[0, q], o.asem.at[1, q])

    def to_cells(self, modes, xi):
        o = self.own
        hi, lo = halves(jnp.concatenate((modes, turn(modes)), axis=0))
        o.vs[...] = dot3(xi, hi, lo).reshape(WIDE, 8, 128)
        o.vr[self.w] = o.vs[self.w]
        self.x.start()

    def gather(self):
        o = self.own
        self.x.arrived()
        tiles = [exchange([o.vr[k * 8 + t] for t in range(8)]) for k in range(KY)]
        for q in range(CHUNKS):
            for k in range(KY):
                for c8 in range(8):
                    o.as_[q, k * XC : k * XC + XC, c8 * 128 : c8 * 128 + 128] = tiles[k][c8][
                        q * XC : q * XC + XC
                    ]
            o.ar[q, self.n] = o.as_[q]
            self.y(q).start(whole=True)

    def chunk(self, q):
        s, o = self.s, self.own
        self.y(q).arrived()
        columns = []
        for c8 in range(8):
            part = o.ar[q, :, :, c8 * 128 : c8 * 128 + 128].reshape(NARROW * ROWS, 128)
            columns.append(jnp.concatenate((part, turn(part)), axis=0))
        hi, lo = halves(jnp.concatenate(columns, axis=1))
        out = dot3(s.yi, hi, lo)
        for i in range(XC):
            for c8 in range(8):
                s.s[pl.ds(i * 256 + c8, YL, stride=8), :] = out[
                    i * YL : i * YL + YL, c8 * 128 : c8 * 128 + 128
                ]

    def field_row(self, i, zi):
        s = self.s
        hi, lo = halves(s.s[pl.ds(pl.multiple_of(i * 256, 256), 256), :])
        both = jnp.concatenate((hi, lo, hi), axis=1)
        for g in range(4):
            s.field[:, g] = dot(both, zi[g]).reshape(YL, 8, NZ)

    def finish(self):
        self.x.sent()
        loop(CHUNKS, lambda q: self.y(q).sent())


def fold_point(full):
    row = lax.broadcasted_iota(jnp.int32, full.shape, 0) // 32
    full = jnp.where(row == lane_of(full.shape) // 32, full, 0.0)
    total = full[0:32]
    for y in range(1, 8):
        total = total + full[y * 32 : y * 32 + 32]
    total = total[:, :128] + total[:, 128:]
    total = total + pltpu.roll(total, 64, 1)
    total = total + pltpu.roll(total, 32, 1)
    lane = lane_of((8, 128))
    low = jnp.where(lane < 32, total[0:8], total[8:16])
    high = jnp.where(lane < 96, total[16:24], total[24:32])
    return jnp.where(lane < 64, low, high)


def gelu_slope(u):
    k = math.sqrt(2.0 / math.pi)
    square = u * u
    h = 0.5 * jnp.tanh(u * (k + (k * 0.044715) * square)) + 0.5
    return h + h * (1.0 - h) * (u * (2.0 * k + (6.0 * k * 0.044715) * square))


def select(rows, pick):
    hi, lo = halves(rows)
    return dot(hi, pick) + dot(lo, pick)


def gather_back(columns, pick):
    hi, lo = halves(columns)
    return dot_t(hi, pick) + dot_t(lo, pick)


def part_of(columns, part, k2):
    at = (2 * part + k2) * 128
    return columns[:, at : at + 128]


def own_channel(rows):
    row = lax.rem(lax.broadcasted_iota(jnp.int32, rows.shape, 0), 8)
    return jnp.where(lane_of(rows.shape) // 16 == row, rows, 0.0)


def over_rows(rows):
    lanes = rows.shape[1]
    return jnp.broadcast_to(rows[:, None], (WIDE, 8, lanes)).reshape(WIDE * 8, lanes)


def by_input(modes, pick_c):
    return select(own_channel(over_rows(modes)), pick_c)


def weight_of(wr):
    def at(part, k2):
        return wr[:, 2 * part + k2].reshape(WIDE * 8, 128)

    return at


def mix_modes(modes, weight, pick_c, pick_o):
    columns = by_input(modes, pick_c)
    real, imag = [], []
    for k2 in range(2):
        c_real, c_imag = part_of(columns, 0, k2), part_of(columns, 1, k2)
        w_real, w_imag = weight(0, k2), weight(1, k2)
        real.append(c_real * w_real - c_imag * w_imag)
        imag.append(c_real * w_imag + c_imag * w_real)
    full = jnp.concatenate(real + imag, axis=1).reshape(WIDE, 8, 512)
    return gather_back(jnp.sum(full, axis=1), pick_o)


def mix_back(grads, weight, pick_c, pick_o):
    columns = over_rows(select(grads, pick_o))
    real, imag = [], []
    for k2 in range(2):
        g_real, g_imag = part_of(columns, 0, k2), part_of(columns, 1, k2)
        w_real, w_imag = weight(0, k2), weight(1, k2)
        real.append(g_real * w_real + g_imag * w_imag)
        imag.append(g_imag * w_real - g_real * w_imag)
    full = own_channel(gather_back(jnp.concatenate(real + imag, axis=1), pick_c))
    return jnp.sum(full.reshape(WIDE, 8, 128), axis=1)


def outer_modes(sg_ref, modes, grads, pick_c, pick_o):
    first = by_input(modes, pick_c)
    second = over_rows(select(grads, pick_o))
    for k2 in range(2):
        c_real, c_imag = part_of(first, 0, k2), part_of(first, 1, k2)
        g_real, g_imag = part_of(second, 0, k2), part_of(second, 1, k2)
        for part, value in enumerate(
            (c_real * g_real + c_imag * g_imag, c_real * g_imag - c_imag * g_real)
        ):
            for g in range(4):
                moved = pltpu.roll(value, (128 - 32 * g) % 128, 1) if g else value
                sg_ref[part, 0, :, :, k2, g * 8 : g * 8 + 8, :] = moved[:, :C].reshape(KY, 8, 8, C)


def pack_weight(s, n, w):
    def one(k):
        for part in range(2):
            for k2 in range(2):
                full = s.weight[part, k, :, k2].astype(F32)
                tile = jnp.concatenate([full[:, g * 8 : g * 8 + 8] for g in range(4)], axis=-1)
                s.ws[pl.ds(pl.multiple_of(k * 8, 8), 8), 2 * part + k2] = tile

    loop(KY, one)
    s.wr[w] = s.ws[w]


def kernel(
    names,
    act_hbm,
    cot_hbm,
    point_ref,
    bias_ref,
    weight_hbm,
    yf_hbm,
    yi_hbm,
    xf_hbm,
    xi_hbm,
    zf_ref,
    ziw_hbm,
    zi1_hbm,
    pick_c_hbm,
    pick_o_hbm,
    out_ref,
    point_grad_ref,
    bias_grad_ref,
    sg_ref,
    *refs,
):
    s = Names(names, refs)
    n, w = lax.axis_index("narrow"), lax.axis_index("wide")

    def group(prefix, keys):
        keys = tuple(keys)
        return Names(keys, [getattr(s, prefix + key) for key in keys])

    ahead = Forward(s, group("f1_", FORWARD), n, w)
    grad = Forward(s, group("f2_", FORWARD), n, w)
    mixed_in = Inverse(s, group("i1_", INVERSE), n, w)
    back_in = Inverse(s, group("i2_", INVERSE), n, w)

    def act_copy(x):
        return pltpu.make_async_copy(act_hbm.at[x], s.act.at[x], s.act_sem.at[x])

    def cot_copy(x):
        return pltpu.make_async_copy(cot_hbm.at[x], s.cot.at[x], s.cot_sem.at[x])

    later = [
        pltpu.make_async_copy(source, target, s.later_sem.at[i])
        for i, (source, target) in enumerate(
            (
                (xf_hbm, s.xf),
                (xi_hbm, s.xi),
                (pick_c_hbm, s.pick_c),
                (pick_o_hbm, s.pick_o),
                (ziw_hbm, s.ziw),
                (zi1_hbm, s.zi1),
            )
        )
    ]
    table_in = [
        pltpu.make_async_copy(yf_hbm.at[n], s.yf, s.table_sem.at[0]),
        pltpu.make_async_copy(yi_hbm.at[n], s.yi, s.table_sem.at[1]),
    ]
    weight_copy = pltpu.make_async_copy(weight_hbm.at[:, 0], s.weight, s.table_sem.at[2])
    weight_copy.start()
    barrier = greet(n, w)
    for copy in table_in:
        copy.start()
    loop(XL, lambda x: act_copy(x).start())
    for copy in later:
        copy.start()
    loop(XL, lambda x: cot_copy(x).start())
    weight_round = Round("wide", WIDE, w, s.ws, s.wr, s.wsem.at[0], s.wsem.at[1])
    weight_copy.wait()
    pack_weight(s, n, w)
    for copy in table_in:
        copy.wait()

    def forward_chunk(q):
        def row(i):
            x = q * XC + i
            act_copy(x).wait()
            ahead.put_rows(i, depth_forward(s.act[x], zf_ref[...]))

        loop(XC, row)

        @pl.when(q == 0)
        def _():
            greeted(barrier)

        ahead.send_chunk(q)

        @pl.when(q == 0)
        def _():
            weight_round.start()

    loop(CHUNKS, forward_chunk)

    row = lax.broadcasted_iota(jnp.int32, (256, 32), 0)
    pick = lax.rem(row, 32) == lane_of((256, 32))
    ones = jnp.where(pick, 1.0, 0.0).astype(BF16)
    bias_rows = jnp.sum(jnp.where(pick, bias_ref[...], 0.0), axis=1, keepdims=True)
    same = lax.broadcasted_iota(jnp.int32, (256, 256), 0) // 32 == lane_of((256, 256)) // 32
    tall = dot(ones, point_ref[...]).astype(BF16)
    s.mix_back[...] = jnp.where(same, dot_t(tall, ones), 0.0).astype(BF16)
    tall = dot_t(ones, point_ref[...]).astype(BF16)
    s.mix[...] = jnp.where(same, dot_t(tall, ones), 0.0).astype(BF16)

    def blocks(fn, low, high):
        def one(i, carry):
            fn(i // 4, pl.ds(pl.multiple_of(lax.rem(i, 4) * 8, 8), 8))
            return carry

        lax.fori_loop(low, high, one, 0)

    def mix_block(x, ys):
        point = dot(s.mix[...], s.act[x, ys].reshape(256, NZ)) + bias_rows
        s.point[x, ys] = point.reshape(8, C, NZ)

    for copy in later:
        copy.wait()
    xf_ref, xi_ref, ziw_ref, zi1_ref = s.xf, s.xi, s.ziw, s.zi1
    pick_c, pick_o = s.pick_c[...], s.pick_o[...]
    weight = weight_of(s.wr)
    blocks(mix_block, 0, 20)
    ahead.sum_chunks()
    blocks(mix_block, 20, 26)
    weight_round.arrived()
    coeffs = ahead.modes(xf_ref)
    mixed_in.to_cells(mix_modes(coeffs, weight, pick_c, pick_o), xi_ref)
    ahead.to_owner(coeffs)
    s.bs[...] = jnp.zeros_like(s.bs)
    s.pg[...] = jnp.zeros_like(s.pg)
    blocks(mix_block, 26, 4 * XL)
    mixed_in.gather()

    def middle_chunk(q):
        mixed_in.chunk(q)

        def row(i):
            x = q * XC + i
            cot_copy(x).wait()
            mixed_in.field_row(i, ziw_ref)

            def block(b):
                ys = pl.ds(pl.multiple_of(b * 8, 8), 8)
                preact = s.field[ys].reshape(256, NZ) + s.point[x, ys].reshape(256, NZ)
                cot = s.cot[x, ys].reshape(256, NZ).astype(F32)
                pre = (cot * gelu_slope(preact)).astype(BF16)
                s.pre[x, ys] = pre.reshape(8, C, NZ)

            loop(4, block)
            depth = depth_forward(s.pre[x], zf_ref[...])
            s.bs[...] += jnp.sum(depth, axis=0)
            grad.put_rows(i, depth)

        loop(XC, row)
        grad.send_chunk(q)

    loop(CHUNKS, middle_chunk)

    def back_block(x, ys):
        pre = s.pre[x, ys].reshape(256, NZ)
        s.pg[...] += dot_t(s.act[x, ys].reshape(256, NZ), pre)
        s.point[x, ys] = dot(s.mix_back[...], pre).reshape(8, C, NZ)

    blocks(back_block, 0, 8)
    grad.sum_chunks()
    blocks(back_block, 8, 20)
    rows = grad.modes(xf_ref)
    first = lax.rem(w, 8) == 0
    grads = rows * jnp.where((lax.rem(lane_of(rows.shape), 2) == 0) & first, 1.0, 2.0)
    back_in.to_cells(mix_back(grads, weight, pick_c, pick_o), xi_ref)
    grad.to_owner(grads)
    blocks(back_block, 20, 4 * XL)
    s.ps[0:8] = fold_point(s.pg[...])
    s.ps[8:16] = s.bs[...]
    s.pr[n] = s.ps[...]
    narrow_sum = Round("narrow", NARROW, n, s.ps, s.pr, s.psem.at[0], s.psem.at[1])
    narrow_sum.start(whole=True)
    back_in.gather()
    outer_modes(sg_ref, ahead.owned(), grad.owned(), pick_c, pick_o)
    narrow_sum.arrived()
    total = s.pr[0]
    for t in range(1, NARROW):
        total = total + s.pr[t]
    s.ts[...] = total
    s.tr[w] = total
    wide_sum = Round("wide", WIDE, w, s.ts, s.tr, s.tsem.at[0], s.tsem.at[1])
    wide_sum.start(whole=True)

    def pointwise_totals():
        wide_sum.arrived()
        total = s.tr[0]
        for t in range(1, WIDE):
            total = total + s.tr[t]
        for g in range(4):
            point_grad_ref[g * 8 : g * 8 + 8] = SCALE * total[0:8, g * 32 : g * 32 + C]
        row, lane = lax.broadcasted_iota(jnp.int32, (8, C), 0), lane_of((8, C))
        bias_grad = jnp.zeros((8, C), F32)
        for g in range(4):
            bias_grad = jnp.where(lane == g * 8 + row, total[8:16, g * 4 : g * 4 + 1], bias_grad)
        bias_grad_ref[...] = SCALE * jnp.sum(bias_grad, axis=0, keepdims=True)

    def last_chunk(q):
        back_in.chunk(q)

        def row(i):
            x = q * XC + i
            back_in.field_row(i, zi1_ref)

            def block(b):
                ys = pl.ds(pl.multiple_of(b * 8, 8), 8)
                out = s.field[ys].reshape(256, NZ) + s.point[x, ys].reshape(256, NZ)
                out_ref[x, ys] = out.astype(BF16).reshape(8, C, NZ)

            loop(4, block)

        loop(XC, row)

    loop(CHUNKS, last_chunk)
    pointwise_totals()
    for part in (ahead, grad, mixed_in, back_in):
        part.finish()
    narrow_sum.sent()
    wide_sum.sent()
    weight_round.sent()


def write_kernel(*refs):
    sources, targets, sems = refs[:4], refs[4:8], refs[8]
    copies = [
        pltpu.make_async_copy(sources[0].at[x], targets[0].at[x], sems.at[x]) for x in range(XL)
    ] + [
        pltpu.make_async_copy(source, target, sems.at[XL + i])
        for i, (source, target) in enumerate(zip(sources[1:], targets[1:]))
    ]
    for copy in copies:
        copy.start()
    for copy in copies:
        copy.wait()


def write_out(*arrays):
    return pl.pallas_call(
        write_kernel,
        name="write_results",
        in_specs=[VM] * 4,
        out_specs=[HB] * 4,
        out_shape=[jax.ShapeDtypeStruct(a.shape, a.dtype) for a in arrays],
        scratch_shapes=[pltpu.SemaphoreType.DMA((XL + 3,))],
        compiler_params=pltpu.CompilerParams(vmem_limit_bytes=1024 * 1024),
    )(*arrays)


VM = pl.BlockSpec(memory_space=pltpu.VMEM)
HB = pl.BlockSpec(memory_space=pl.ANY)
FIELD = (XL, YL, C, NZ)


def local(activations, cotangent, point_weight, bias, spectral_weight):
    tabs = {name: jnp.asarray(value) for name, value in tables().items()}
    scratch = dict(
        act=pltpu.VMEM(FIELD, BF16),
        cot=pltpu.VMEM(FIELD, BF16),
        pre=pltpu.VMEM(FIELD, BF16),
        point=pltpu.VMEM(FIELD, F32),
        field=pltpu.VMEM((YL, 4, 8, NZ), F32),
        d=pltpu.VMEM((256, 128), F32),
        rh=pltpu.VMEM((64 * XC, 1024), BF16),
        rl=pltpu.VMEM((64 * XC, 1024), BF16),
        s=pltpu.VMEM((XC * 256, 128), F32),
        yf=pltpu.VMEM((2, 32 * XC, 64 * XC), BF16),
        yi=pltpu.VMEM((2, 32 * XC, 64 * XC), BF16),
        xf=pltpu.VMEM((2, 32, 512), BF16),
        xi=pltpu.VMEM((2, 256, 64), BF16),
        pick_c=pltpu.VMEM((128, 512), BF16),
        pick_o=pltpu.VMEM((128, 512), BF16),
        ziw=pltpu.VMEM((4, 384, NZ), BF16),
        zi1=pltpu.VMEM((4, 384, NZ), BF16),
        later_sem=pltpu.SemaphoreType.DMA((6,)),
        mix=pltpu.VMEM((256, 256), BF16),
        mix_back=pltpu.VMEM((256, 256), BF16),
        weight=pltpu.VMEM((2, KY, 8, 2, C, C), BF16),
        ws=pltpu.VMEM((WIDE, 4, 8, 128), F32),
        wr=pltpu.VMEM((WIDE, 4, 8, 128), F32),
        pg=pltpu.VMEM((256, 256), F32),
        bs=pltpu.VMEM((8, 128), F32),
        ps=pltpu.VMEM((16, 128), F32),
        pr=pltpu.VMEM((NARROW, 16, 128), F32),
        ts=pltpu.VMEM((16, 128), F32),
        tr=pltpu.VMEM((WIDE, 16, 128), F32),
        act_sem=pltpu.SemaphoreType.DMA((XL,)),
        cot_sem=pltpu.SemaphoreType.DMA((XL,)),
        table_sem=pltpu.SemaphoreType.DMA((4,)),
        wsem=pltpu.SemaphoreType.DMA((2,)),
        psem=pltpu.SemaphoreType.DMA((2,)),
        tsem=pltpu.SemaphoreType.DMA((2,)),
    )
    for prefix, group in (("f1_", FORWARD), ("f2_", FORWARD), ("i1_", INVERSE), ("i2_", INVERSE)):
        scratch.update({prefix + key: value for key, value in group.items()})
    input_grad, point_grad, bias_grad, spectral_grad = pl.pallas_call(
        functools.partial(kernel, tuple(scratch)),
        name="layer_backward",
        in_specs=[HB, HB, VM, VM, HB, HB, HB, HB, HB, VM, HB, HB, HB, HB],
        out_specs=[VM, VM, VM, VM],
        out_shape=[
            pltpu.VMEM(FIELD, BF16),
            pltpu.VMEM((C, C), F32),
            pltpu.VMEM((1, C), F32),
            pltpu.VMEM((2, 1, KY, 8, 2, C, C), F32),
        ],
        scratch_shapes=tuple(scratch.values()),
        compiler_params=pltpu.CompilerParams(
            collective_id=0, has_side_effects=True, vmem_limit_bytes=48 * 1024 * 1024
        ),
    )(
        activations,
        cotangent,
        point_weight,
        bias[None],
        spectral_weight.reshape(2, 1, KY, 8, 2, C, C),
        *(tabs[name] for name in ("yf", "yi", "xf", "xi", "zf", "ziw", "zi1", "pick_c", "pick_o")),
    )

    input_grad, point_grad, bias_grad, spectral_grad = write_out(
        input_grad, point_grad, bias_grad, spectral_grad
    )
    spectral_grad = spectral_grad.reshape(2, 1, KY, M, C, C)
    return (input_grad, point_grad, bias_grad.reshape(C), spectral_grad)


def solution(mesh):
    return jax.shard_map(
        local,
        mesh=mesh,
        in_specs=(
            P("wide", "narrow", None, None),
            P("wide", "narrow", None, None),
            P(),
            P(),
            P(None, "wide", "narrow", None, None, None),
        ),
        out_specs=(
            P("wide", "narrow", None, None),
            P(),
            P(),
            P(None, "wide", "narrow", None, None, None),
        ),
        check_vma=False,
    )
```
